512 devices in a mesh: kv: 16 (over y, core), tp: 32 (over x, z).
Axes of the slice: x: 4, y: 8, z: 8, core: 2. Of those that a mesh axis runs over, the one named last changes fastest.
Arguments:
- tokens: bfloat16 [256, 7168], P('tp', 'kv'), may hold values from -8 to 8
- attn_gain: float32 [7168], P('kv'), may hold values from 0.5 to 1.5
- down_kv: bfloat16 [7168, 576], P('kv'), may hold values from -0.0625 to 0.0625
- latent_gain: float32 [512], replicated, may hold values from 0.5 to 1.5
- query_nope: bfloat16 [256, 16384], P(None, 'tp'), may hold values from -8 to 8
- query_rope: bfloat16 [256, 8192], P(None, 'tp'), may hold values from -8 to 8
- cache: bfloat16 [2, 12288, 576], P(None, 'kv'), may hold values from -6 to 6
- lengths: int32 [2], replicated, may hold values from 3072 to 12288, as said below
- key_up: bfloat16 [128, 128, 512], P('tp', None, 'kv'), may hold values from -0.5 to 0.5
- value_up: bfloat16 [128, 512, 128], P('tp', 'kv'), may hold values from -0.25 to 0.25
- out_proj: bfloat16 [16384, 7168], P('tp', 'kv'), may hold values from -0.1875 to 0.1875
- mlp_gain: float32 [7168], P('kv'), may hold values from 0.5 to 1.5
- expert_ids: int32 [256, 8], P('tp'), may hold values from 0 to 15, all different within a row; in each aligned block of 8 rows (0 to 7, 8 to 15, ...) at most 6 rows name the same one
- expert_weights: float32 [256, 8], P('tp'), may hold values from 0.1 to 1
- gate_proj: bfloat16 [32, 7168, 1024], P('tp', 'kv'), may hold values from -0.0625 to 0.0625
- up_proj: bfloat16 [32, 7168, 1024], P('tp', 'kv'), may hold values from -0.0625 to 0.0625
- down_proj: bfloat16 [32, 1024, 7168], P('tp', None, 'kv'), may hold values from -0.125 to 0.125
Outputs:
- attended: bfloat16 [256, 7168], P('tp', 'kv')
- mixed: bfloat16 [256, 7168], P('tp', 'kv')
The draws below stay inside these ranges and needn't reach their ends.
Inputs may be any that keep to these rules, and one draw needn't show every extreme that they name: `expert_ids`: in each aligned block of 8 rows (the rows of one index of tp) no expert is named by more than 6 rows, a bound that some block reaches; a row names 8 different experts. `lengths`: some sequence has all 12288 positions.
All inputs are finite; a program needn't handle non-finite values.
Results may differ from the reference program's by a relative error of at most 0.011.
Values may be sent and summed in bfloat16 or wider, within the bound.
No kernel may reach another device: no remote copies, remote signals or barrier semaphores. Data moves between devices by JAX's collectives and lax.ppermute only.
A program may use at most 128 MiB of HBM per device.

```python
import math
import jax
import jax.numpy as jnp
import numpy as np
from jax import lax

D = 7168
HEADS = 128
NOPE = 128
ROPE = 64
LAT = 512
VDIM = 128
FFE = 2048
CACHE_DEV = 768
SEQS = 2
QROWS = 32
STEPS = 4
LENGTH = 12288
TOKROWS = 256
ROWS_TP = 8
EXPERTS = 16
TOPK = 8
CAP = 6
N_KV = 16


def draw_tokens(key, part):
    key = jax.random.fold_in(key, 3)
    keys = jax.random.split(key, 3)
    row_scale = jnp.exp(jax.random.uniform(keys[0], (TOKROWS, 1), minval=math.log(0.3), maxval=math.log(3.0)))
    column_scale = jnp.exp(jax.random.uniform(keys[1], (1, D), minval=math.log(0.3), maxval=math.log(3.0)))
    across = jnp.arange(D, dtype=jnp.float32)[None, :] / (D - 1)
    values = jax.random.normal(keys[2], (TOKROWS, D)) * row_scale * column_scale * 3.0 ** across / 5.0
    return jnp.clip(values, -8.0, 8.0).astype(jnp.bfloat16)


def draw_cache(key, part):
    key = jax.random.fold_in(key, 5)
    values = jnp.clip(jax.random.normal(key, (SEQS, LENGTH, LAT + ROPE)), -6.0, 6.0)
    return values.astype(jnp.bfloat16)


def draw_query_rope(key, part):
    key = jax.random.fold_in(key, 7)
    values = jnp.clip(jax.random.normal(key, (TOKROWS, HEADS * ROPE)), -8.0, 8.0)
    return values.astype(jnp.bfloat16)


def draw_lengths(key, part):
    key = jax.random.fold_in(key, 9)
    keys = jax.random.split(key, 2)
    drawn = jax.random.randint(keys[0], (SEQS,), LENGTH // 4, LENGTH + 1)
    longest = jax.random.randint(keys[1], (), 0, SEQS)
    return jnp.where(jnp.arange(SEQS, dtype=jnp.int32) == longest, LENGTH, drawn).astype(jnp.int32)


def levels(stream_key, dims, cuts, low, top_value):
    loudness = 1.0
    for dim, parts in cuts:
        steps = jax.random.uniform(jax.random.fold_in(jax.random.fold_in(stream_key, 6), dim), (parts,), jnp.float32, low / len(cuts), top_value / len(cuts))
        loudness = loudness * jnp.repeat(jnp.exp(steps), dims[dim] // parts).reshape((-1,) + (1,) * (len(dims) - 1 - dim))
    return loudness


def assign_block(key, own, number, rows, number_of, top, limit, slope):
    order = jax.random.permutation(key, number_of)
    crowded, usual = load_shares(number_of, rows * top, limit, slope, True), load_shares(number_of, rows * top, limit, slope, False)
    places = jnp.arange(number_of)

    def named(sizes, rotation):
        used = int((sizes > 0).sum())
        fixed = max(1, used // 4)
        passed = fixed + (places - fixed + rotation * (used - fixed)) % max(1, number_of - fixed)
        return jnp.zeros((number_of,), jnp.int32).at[order[jnp.where(places < fixed, places, passed)]].set(jnp.asarray(sizes, jnp.int32))

    sizes = jnp.where(number % 4 == 0, named(crowded, number // 4), named(usual, number - number // 4 - 1))
    mixed = jax.random.permutation(jax.random.fold_in(own, 3), number_of)
    source_of, receiver = mixed[0:number_of // 2 * 2:2], mixed[1:number_of // 2 * 2:2]
    margin = jnp.minimum(sizes[source_of] - 1, limit - sizes[receiver]) // 2
    margin = jnp.where((source_of == order[0]) | (receiver == order[0]) | (sizes[receiver] == 0), 0, jnp.maximum(margin, 0))
    passed = jax.random.randint(jax.random.fold_in(own, 4), (number_of // 2,), 0, 1 << 20) % (margin + 1)
    sizes = sizes.at[source_of].add(-passed).at[receiver].add(passed)
    members = jnp.searchsorted(jnp.cumsum(sizes), jnp.arange(rows * top), side="right").astype(jnp.int32)
    grid = members.reshape(top, rows).T
    grid = grid[jax.random.permutation(jax.random.fold_in(own, 1), rows)]
    rotation = jax.random.randint(jax.random.fold_in(own, 2), (rows, 1), 0, top)
    return jnp.take_along_axis(grid, (jnp.arange(top)[None, :] + rotation) % top, axis=1)


def load_shares(count, total, reach, skew, full):
    loads = [(1 << 20) // math.isqrt(rank ** skew) + 1 for rank in range(1, count + 1)]
    largest = reach if full else min(reach, max(-(-total // count), total * loads[0] // sum(loads)))
    least = 1 if total - largest >= count - 1 else 0
    given, surplus = [largest] + [least] * (count - 1), total - largest - least * (count - 1)
    while surplus > 0:
        movable = [i for i in range(1, count) if given[i] < largest] or [i for i in range(1, count) if given[i] < reach]
        whole, remaining = sum([loads[i] for i in movable]), surplus
        for i in movable:
            more = min(reach - given[i], max(1, remaining * loads[i] // whole), surplus)
            given[i] = given[i] + more
            surplus = surplus - more
    return np.array(given)


def scatter_about(rng, dims, deviation, limit, pieces=(), kind=jnp.bfloat16):
    level = levels(rng, dims, pieces, -0.22, 0.18) if pieces else 1.0
    values = jax.random.normal(rng, dims, jnp.float32) * deviation * level
    return jnp.minimum(jnp.maximum(values, -limit), limit).astype(kind)


def setup_inputs(seed: int = 0) -> dict:
    streams_of = jax.random.split(jax.random.key(seed), 18)
    tokens = draw_tokens(jax.random.fold_in(streams_of[17], 71), 0)
    attn_gain = jnp.clip(1.0 + 0.1 * jax.random.normal(streams_of[1], (D,), jnp.float32), 0.5, 1.5)
    down_kv = scatter_about(streams_of[2], (D, LAT + ROPE), D ** -0.5, 0.0625, ((0, 16),))
    latent_gain = jnp.clip(1.0 + 0.1 * jax.random.normal(streams_of[3], (LAT,), jnp.float32), 0.5, 1.5)
    query_nope = scatter_about(streams_of[4], (TOKROWS, HEADS * NOPE), 1.0, 8.0, ((1, 32),))
    query_rope = draw_query_rope(jax.random.fold_in(streams_of[17], 71), 0)
    cache = draw_cache(jax.random.fold_in(streams_of[17], 71), 0)
    lengths = draw_lengths(jax.random.fold_in(streams_of[17], 71), 0)
    key_up = scatter_about(streams_of[8], (HEADS, NOPE, LAT), NOPE ** -0.5, 0.5, ((0, 32), (2, 16)))
    value_up = scatter_about(streams_of[9], (HEADS, LAT, VDIM), LAT ** -0.5, 0.25, ((0, 32), (1, 16)))
    out_proj = scatter_about(streams_of[10], (HEADS * VDIM, D), (HEADS * VDIM // 16) ** -0.5, 0.1875, ((0, 32), (1, 16)))
    mlp_gain = jnp.clip(1.0 + 0.1 * jax.random.normal(streams_of[11], (D,), jnp.float32), 0.5, 1.5)
    expert_ids_keys = jax.random.split(jax.random.fold_in(streams_of[12], 1), TOKROWS // ROWS_TP)
    expert_ids_turns = jax.random.permutation(jax.random.fold_in(streams_of[12], 3), TOKROWS // ROWS_TP)
    expert_ids = jax.vmap(lambda own, number: assign_block(jax.random.fold_in(streams_of[12], 2), own, number, ROWS_TP, EXPERTS, TOPK, CAP, 1))(expert_ids_keys, expert_ids_turns).reshape((TOKROWS, TOPK))
    expert_weights = jnp.clip(jnp.exp(math.log(1.0) - 2.3025851 * jax.random.uniform(streams_of[13], (TOKROWS, TOPK), jnp.float32) ** levels(streams_of[13], (TOKROWS, TOPK), ((0, 32),), -0.2, 0.2)), 0.1, 1.0)
    gate_proj = scatter_about(streams_of[14], (2 * EXPERTS, D, FFE // 2), D ** -0.5, 0.0625, ((0, 32), (1, 16)))
    up_proj = scatter_about(streams_of[15], (2 * EXPERTS, D, FFE // 2), D ** -0.5, 0.0625, ((0, 32), (1, 16)))
    down_proj = scatter_about(streams_of[16], (2 * EXPERTS, FFE // 2, D), FFE ** -0.5, 0.125, ((0, 32), (2, 16)))
    return dict(tokens=tokens, attn_gain=attn_gain, down_kv=down_kv, latent_gain=latent_gain, query_nope=query_nope, query_rope=query_rope, cache=cache, lengths=lengths, key_up=key_up, value_up=value_up, out_proj=out_proj, mlp_gain=mlp_gain, expert_ids=expert_ids, expert_weights=expert_weights, gate_proj=gate_proj, up_proj=up_proj, down_proj=down_proj)


EPS = 1e-06
LOWEST = -1e+30

def normalize(values, gain):
    return values * lax.rsqrt(lax.optimization_barrier(jnp.mean(values * values, axis=-1, keepdims=True)) + EPS) * gain

def rotate(part, positions):
    half = part.shape[-1] // 2
    freq = 10000.0 ** (-2.0 * jnp.arange(half, dtype=jnp.float32) / part.shape[-1])
    angle = positions.astype(jnp.float32)[..., None] * freq
    cosine = jnp.cos(angle)
    sine = jnp.sin(angle)
    first = part[..., :half]
    second = part[..., half:]
    return jnp.concatenate([first * cosine - second * sine, second * cosine + first * sine], axis=-1)

def rounded(values):
    return lax.optimization_barrier(values.astype(jnp.bfloat16)).astype(jnp.float32)

def reference(tokens, attn_gain, down_kv, latent_gain, query_nope, query_rope, cache, lengths, key_up, value_up, out_proj, mlp_gain, expert_ids, expert_weights, gate_proj, up_proj, down_proj):
    scale = 1.0 / math.sqrt(NOPE + ROPE)
    width = LAT + ROPE
    wide_tokens = tokens.astype(jnp.float32)
    normed = (wide_tokens * attn_gain).astype(jnp.bfloat16)
    fresh = jnp.dot(normed, down_kv, preferred_element_type=jnp.float32)
    row_ids = jnp.arange(TOKROWS, dtype=jnp.int32)
    step_of = row_ids // (SEQS * QROWS)
    seq_of = row_ids // QROWS % SEQS
    seq_labels = jnp.arange(SEQS, dtype=jnp.int32)
    positions = lax.optimization_barrier(jnp.sum(jnp.where(seq_of[:, None] == seq_labels[None, :], lengths[None, :], 0), axis=1)) + step_of
    fresh_key = jnp.concatenate([normalize(fresh[:, :LAT], latent_gain), rotate(fresh[:, LAT:], positions)], axis=1).astype(jnp.bfloat16)
    absorbed = jnp.einsum('rhn,hnl->rhl', query_nope.reshape(TOKROWS, HEADS, NOPE).astype(jnp.float32), key_up.astype(jnp.float32)).astype(jnp.bfloat16)
    queries = jnp.concatenate([absorbed, query_rope.reshape(TOKROWS, HEADS, ROPE)], axis=2)
    query_count = STEPS * QROWS * HEADS
    seq_queries = queries.reshape(STEPS, SEQS, QROWS, HEADS, width).transpose(1, 0, 2, 3, 4).reshape(SEQS, query_count, width).astype(jnp.float32)
    blocks = cache.reshape(SEQS, N_KV, CACHE_DEV, width).transpose(1, 0, 2, 3)

    def sweep(carry, inputs):
        best, total, weighted = carry
        block, index = inputs
        keys = block.astype(jnp.float32)
        scores = jnp.einsum('bqc,btc->bqt', seq_queries, keys) * scale
        places = index * CACHE_DEV + jnp.arange(CACHE_DEV, dtype=jnp.int32)
        valid = (places[None, :] < lengths[:, None])[:, None, :]
        peak = lax.optimization_barrier(jnp.max(jnp.where(valid, scores, LOWEST), axis=2))
        weights = rounded(jnp.where(valid, jnp.exp(scores - peak[..., None]), 0.0))
        part_total = lax.optimization_barrier(jnp.sum(weights, axis=2))
        part_latent = jnp.einsum('bqt,btc->bqc', weights, keys[..., :LAT])
        top = jnp.maximum(best, peak)
        old_keep = jnp.exp(best - top)
        new_keep = jnp.exp(peak - top)
        return ((top, total * old_keep + part_total * new_keep, weighted * old_keep[..., None] + part_latent * new_keep[..., None]), None)
    start = (jnp.full((SEQS, query_count), LOWEST, jnp.float32), jnp.zeros((SEQS, query_count), jnp.float32), jnp.zeros((SEQS, query_count, LAT), jnp.float32))
    (best, total, weighted), _ = lax.scan(sweep, start, (blocks, jnp.arange(N_KV, dtype=jnp.int32)))
    fresh_blocks = fresh_key.reshape(STEPS, SEQS, QROWS, width).astype(jnp.float32)
    step_queries = queries.reshape(STEPS, SEQS, QROWS, HEADS, width).astype(jnp.float32)
    fresh_scores = jnp.einsum('sbjhc,tbjc->sbjht', step_queries, fresh_blocks) * scale
    step_ids = jnp.arange(STEPS, dtype=jnp.int32)
    causal = (step_ids[None, :] <= step_ids[:, None])[:, None, None, None, :]
    fresh_peak = lax.optimization_barrier(jnp.max(jnp.where(causal, fresh_scores, LOWEST), axis=4))
    fresh_weights = rounded(jnp.where(causal, jnp.exp(fresh_scores - fresh_peak[..., None]), 0.0))
    fresh_total = lax.optimization_barrier(jnp.sum(fresh_weights, axis=4))
    fresh_latent = jnp.einsum('sbjht,tbjc->sbjhc', fresh_weights, fresh_blocks[..., :LAT])
    fresh_peak = fresh_peak.transpose(1, 0, 2, 3).reshape(SEQS, query_count)
    fresh_total = fresh_total.transpose(1, 0, 2, 3).reshape(SEQS, query_count)
    fresh_latent = fresh_latent.transpose(1, 0, 2, 3, 4).reshape(SEQS, query_count, LAT)
    top = jnp.maximum(best, fresh_peak)
    keep = jnp.exp(best - top)
    fresh_keep = jnp.exp(fresh_peak - top)
    total_all = total * keep + fresh_total * fresh_keep
    latent_all = weighted * keep[..., None] + fresh_latent * fresh_keep[..., None]
    attn_lat = latent_all / total_all[..., None]
    attn_rows = attn_lat.reshape(SEQS, STEPS, QROWS, HEADS, LAT).transpose(1, 0, 2, 3, 4).reshape(TOKROWS, HEADS, LAT)
    values = jnp.einsum('rhl,hlv->rhv', attn_rows, value_up.astype(jnp.float32), precision=lax.Precision.HIGHEST).reshape(TOKROWS, HEADS * VDIM).astype(jnp.bfloat16)
    attended = jnp.dot(values, out_proj, preferred_element_type=jnp.float32).astype(jnp.bfloat16)
    mid = wide_tokens + attended.astype(jnp.float32)
    mlp_in = normalize(mid, mlp_gain).astype(jnp.bfloat16)
    expert_labels = jnp.arange(EXPERTS, dtype=jnp.int32)
    coeff = lax.optimization_barrier(jnp.sum(jnp.where(expert_ids[:, :, None] == expert_labels[None, None, :], expert_weights[:, :, None], 0.0), axis=1))
    gates = gate_proj.reshape(EXPERTS, 2, D, FFE // 2)
    ups = up_proj.reshape(EXPERTS, 2, D, FFE // 2)
    downs = down_proj.reshape(EXPERTS, 2, FFE // 2, D)

    def one_expert(carry, inputs):
        gate_w, up_w, down_w, column = inputs
        gate = jnp.dot(mlp_in, jnp.concatenate([gate_w[0], gate_w[1]], axis=1), preferred_element_type=jnp.float32)
        upward = jnp.dot(mlp_in, jnp.concatenate([up_w[0], up_w[1]], axis=1), preferred_element_type=jnp.float32)
        hidden = (jax.nn.silu(gate) * upward).astype(jnp.bfloat16)
        produced = jnp.dot(hidden, jnp.concatenate([down_w[0], down_w[1]], axis=0), preferred_element_type=jnp.float32)
        return (carry + column[:, None] * produced, None)
    moe, _ = lax.scan(one_expert, jnp.zeros((TOKROWS, D), jnp.float32), (gates, ups, downs, coeff.T))
    mixed = (mid + moe).astype(jnp.bfloat16)
    return (attended, mixed)
```

```python
import functools
import math

import jax
import jax.numpy as jnp
from jax import lax
from jax.experimental import pallas as pl
from jax.experimental.pallas import tpu as pltpu
from jax.sharding import PartitionSpec as P

D = 7168
NOPE = 128
ROPE = 64
LAT = 512
VDIM = 128
SEQS = 2
QROWS = 32
STEPS = 4
TOKROWS = 256
EXPERTS = 16

N_KV = 16
N_TP = 32
HEADS_DEV = 4
FEAT = D // N_KV
ROWS_TP = TOKROWS // N_TP
ROWS_KV = TOKROWS // N_KV
KEY = LAT + ROPE
PAIRS = SEQS * QROWS
STAT = 2 * HEADS_DEV
ATT_W = LAT + 128
CHIPS = N_KV // 2
LAT_KV = LAT // N_KV
UP_ROWS = 2 * HEADS_DEV * LAT_KV
FRESH_W = KEY + ROPE
FRESH_ROWS = 48
CLASS = TOKROWS // 2
PART_ROWS = 2 * CLASS + 16
KEY_W = 384
HID = 1024
HID_Y = HID // 8

EPS = 1e-06
LOWEST = -1e30
SCALE = 1.0 / math.sqrt(NOPE + ROPE)

F32 = jnp.float32
BF16 = jnp.bfloat16
NT = (((1,), (1,)), ((), ()))
TN = (((0,), (0,)), ((), ()))


def kv_index():
    return lax.axis_index("kv")


def tp_index():
    return lax.axis_index("tp")


def iota(shape, dim):
    return lax.broadcasted_iota(jnp.int32, shape, dim)


def dot(a, b, dims=(((1,), (0,)), ((), ()))):
    return lax.dot_general(a, b, dims, preferred_element_type=F32)


def parts_of(value):
    high = value.astype(BF16).astype(F32)
    rest = value - high
    middle = rest.astype(BF16).astype(F32)
    return high, middle, rest - middle


def with_stats(stats, head, peak, total):
    lane = iota(stats.shape, 1)
    for at, part in enumerate(parts_of(peak)):
        stats = jnp.where(lane == at * STAT + head, part, stats)
    for at, part in enumerate(parts_of(total)):
        stats = jnp.where(lane == at * STAT + HEADS_DEV + head, part, stats)
    return stats


def whole_stats(tail):
    return tail[..., :STAT] + tail[..., STAT : 2 * STAT] + tail[..., 2 * STAT : 3 * STAT]


def by_pair(transposed):
    shape = (TOKROWS, TOKROWS)
    paired, stepped = iota(shape, 1 if transposed else 0), iota(shape, 0 if transposed else 1)
    return (stepped == paired % STEPS * PAIRS + paired // STEPS).astype(F32).astype(BF16)


def swap_halves(rows):
    return pltpu.roll(rows, 4, 0)


def start_kernel(tokens_ref, gain_ref, down_ref, key_ref, value_ref, mlp_gain_ref, out_ref, mine_ref):
    wide_tokens = tokens_ref[...].astype(F32)
    mine_ref[...] = jnp.concatenate([wide_tokens, jnp.broadcast_to(mlp_gain_ref[...], (8, FEAT))], axis=0)
    normed = (wide_tokens * gain_ref[...]).astype(BF16)
    fresh = dot(normed, down_ref[...])
    fresh = jnp.concatenate([fresh, jnp.zeros((ROWS_TP, ROPE), F32)], axis=1)
    tiles = [fresh[:, at * 128 : (at + 1) * 128] for at in range(FRESH_W // 128)]
    tiles.append(jnp.zeros((FRESH_ROWS - ROWS_TP * len(tiles), 128), F32))
    packed = jnp.concatenate(tiles, axis=0).astype(BF16)
    for place in range(CHIPS):
        for head in range(HEADS_DEV):
            out_ref[place, head * LAT_KV : (head + 1) * LAT_KV, :] = key_ref[head]
            out_ref[place, UP_ROWS // 2 + head * LAT_KV : UP_ROWS // 2 + (head + 1) * LAT_KV, :] = value_ref[head]
        out_ref[place, UP_ROWS:, :] = packed


def sum_kernel(ups_ref, out_ref):
    out_ref[...] = jnp.sum(ups_ref[:, UP_ROWS:, :].astype(F32), axis=0)


def fresh_kernel(own_ref, other_ref, gain_ref, lengths_ref, freq_ref, out_ref):
    packed = own_ref[...] + other_ref[...]
    tiles = [packed[at * ROWS_TP : (at + 1) * ROWS_TP] for at in range(FRESH_W // 128)]
    fresh = jnp.concatenate(tiles[:-1], axis=1)
    turn = tiles[-1][:, :ROPE]
    scaled = fresh * lax.rsqrt(jnp.mean(fresh * fresh, axis=1, keepdims=True) + EPS) * gain_ref[...]
    row = tp_index() * ROWS_TP
    lengths = lengths_ref[...]
    start = jnp.where(row // QROWS % SEQS == 0, lengths[:, 0:1], lengths[:, 1:2])
    angle = (start + row // PAIRS).astype(F32) * freq_ref[...]
    cosine, sine = jnp.cos(angle), jnp.sin(angle)
    first, second = turn[:, : ROPE // 2], turn[:, ROPE // 2 :]
    turned = [first * cosine - second * sine, second * cosine + first * sine]
    key = jnp.concatenate([scaled] + turned + [jnp.zeros((ROWS_TP, ROPE), F32)], axis=1)
    key = jnp.where(kv_index() % 2 == 0, key, swap_halves(key))
    upper = jnp.concatenate([key[:, :256], key[:, LAT:]], axis=1)
    lower = jnp.concatenate([swap_halves(key[:, 256:LAT]), jnp.zeros((ROWS_TP, KEY_W - 256), F32)], axis=1)
    key = jnp.where(iota(upper.shape, 0) < ROWS_TP // 2, upper, lower).astype(BF16)
    for place in range(N_TP):
        out_ref[place] = key


def attend_kernel(
    lengths_ref, own_ups_ref, other_ups_ref, nope_ref, rope_ref, keys_ref,
    out_ref, own_ref, ups_ref, queries,
):
    core = kv_index() % 2
    rows_seq = TOKROWS // SEQS
    for source, whose in ((own_ups_ref, core), (other_ups_ref, 1 - core)):
        for chip in range(CHIPS):
            for which in range(2 * HEADS_DEV):
                ups_ref[which, 2 * chip + whose] = source[chip, which * LAT_KV : (which + 1) * LAT_KV, :]
    reorder = by_pair(False)
    nope = dot(reorder, nope_ref[...]).astype(BF16)
    rope = dot(reorder, rope_ref[...]).astype(BF16)
    for head in range(HEADS_DEV):
        key_up = ups_ref[head].reshape(LAT, NOPE)
        absorbed = dot(nope[:, head * NOPE : (head + 1) * NOPE], key_up, NT).astype(BF16)
        turned = rope[:, head * ROPE : (head + 1) * ROPE]
        for seq in range(SEQS):
            rows = slice(seq * rows_seq, (seq + 1) * rows_seq)
            place = slice(head * rows_seq, (head + 1) * rows_seq)
            queries[seq, place, :LAT] = absorbed[rows]
            queries[seq, place, LAT:] = turned[rows]
    own_seq = kv_index() // (N_KV // SEQS)
    own_row = kv_index() % (N_KV // SEQS) * ROWS_KV
    for head in range(HEADS_DEV):
        start = pl.multiple_of(head * rows_seq + own_row, ROWS_KV)
        own_ref[head * ROWS_KV : (head + 1) * ROWS_KV, :] = queries[own_seq, pl.ds(start, ROWS_KV), :]
    span = keys_ref.shape[2]
    lengths = lengths_ref[...]
    for seq in range(SEQS):
        valid = kv_index() * span + iota((1, span), 1) < lengths[:, seq : seq + 1]
        scores = dot(queries[seq], keys_ref[seq]) * SCALE + jnp.where(valid, 0.0, LOWEST)
        peak = jnp.max(scores, axis=1, keepdims=True)
        weights = jnp.where(valid, jnp.exp(scores - peak), 0.0).astype(BF16)
        total = jnp.sum(weights.astype(F32), axis=1, keepdims=True)
        latent = dot(weights, keys_ref[seq, :LAT, :], NT).astype(BF16)
        stats = jnp.zeros((rows_seq, 128), F32)
        rows = slice(seq * rows_seq, (seq + 1) * rows_seq)
        for head in range(HEADS_DEV):
            place = slice(head * rows_seq, (head + 1) * rows_seq)
            value_up = ups_ref[HEADS_DEV + head].reshape(LAT, VDIM)
            out_ref[rows, head * VDIM : (head + 1) * VDIM] = dot(latent[place], value_up).astype(BF16)
            stats = with_stats(stats, head, peak[place], total[place])
        out_ref[rows, LAT:] = stats.astype(BF16)


def merge_kernel(parts_ref, own_ref, ups_ref, keys_ref, out_ref):
    kv = kv_index()
    out_ref[...] = parts_ref[...]
    rows = pl.ds(pl.multiple_of(kv * ROWS_KV, ROWS_KV), ROWS_KV)
    mine = parts_ref[rows, :].astype(F32)
    stats = whole_stats(mine[:, LAT:])
    keys = []
    for step in range(STEPS):
        block = keys_ref[step * (PAIRS // ROWS_TP) + kv // 2].astype(F32)
        keys.append(jnp.concatenate([block[:, :256], swap_halves(block[:, :256]), block[:, 256 : 256 + ROPE]], axis=1))
    keys = jnp.concatenate(keys, axis=0).astype(BF16)
    scores = dot(own_ref[...], keys, NT) * SCALE
    row = iota(scores.shape, 0) % ROWS_KV
    key = iota(scores.shape, 1)
    causal = (row // STEPS == key % ROWS_TP) & (key // ROWS_TP <= row % STEPS)
    scores = jnp.where(causal, scores, LOWEST)
    fresh_peak = jnp.max(scores, axis=1, keepdims=True)
    weights = jnp.where(causal, jnp.exp(scores - fresh_peak), 0.0).astype(BF16)
    fresh_total = jnp.sum(weights.astype(F32), axis=1, keepdims=True)
    fresh_latent = dot(weights, keys[:, :LAT]).astype(BF16)
    tail = jnp.zeros((ROWS_KV, 128), F32)
    merged = []
    for head in range(HEADS_DEV):
        own = slice(head * ROWS_KV, (head + 1) * ROWS_KV)
        peak = stats[:, head : head + 1]
        top = jnp.maximum(peak, fresh_peak[own])
        keep = jnp.exp(peak - top)
        fresh_keep = jnp.exp(fresh_peak[own] - top)
        value_up = ups_ref[HEADS_DEV + head].reshape(LAT, VDIM)
        part = mine[:, head * VDIM : (head + 1) * VDIM]
        merged.append(part * keep + dot(fresh_latent[own], value_up) * fresh_keep)
        total = stats[:, HEADS_DEV + head : HEADS_DEV + head + 1] * keep + fresh_total[own] * fresh_keep
        tail = with_stats(tail, head, top, total)
    out_ref[rows, :] = jnp.concatenate(merged + [tail], axis=1).astype(BF16)


def combine_kernel(parts_ref, out_ref):
    stats = whole_stats(parts_ref[:, :, LAT:].astype(F32))
    for head in range(HEADS_DEV):
        peak = stats[:, :, head : head + 1]
        total = stats[:, :, HEADS_DEV + head : HEADS_DEV + head + 1]
        keep = jnp.exp(peak - jnp.max(peak, axis=0, keepdims=True))
        part = parts_ref[:, :, head * VDIM : (head + 1) * VDIM].astype(F32)
        value = jnp.sum(part * keep, axis=0) / jnp.sum(total * keep, axis=0)
        for place in range(CHIPS):
            out_ref[place, :, head * VDIM : (head + 1) * VDIM] = value.astype(BF16)


def own_half(shape, dim):
    return iota(shape, dim) % ROWS_TP // (ROWS_TP // 2) == kv_index() % 2


def project_kernel(values_ref, own_ref, other_ref, out_ref):
    values = values_ref[...].reshape(CLASS, HEADS_DEV * VDIM)
    shape = (TOKROWS, CLASS)
    row, source = iota(shape, 0), iota(shape, 1)
    block, pair = row // ROWS_TP, row % (ROWS_TP // 2)
    match = source == block % CHIPS * ROWS_KV + pair * STEPS + block // CHIPS
    own = (match & own_half(shape, 0)).astype(F32).astype(BF16)
    other = (match & ~own_half(shape, 0)).astype(F32).astype(BF16)
    out = dot(dot(own, values).astype(BF16), own_ref[...], NT)
    out = out + dot(dot(other, values).astype(BF16), other_ref[...], NT)
    out_ref[...] = out.reshape(N_TP, ROWS_TP, FEAT).astype(BF16)


def route_kernel(parts_ref, mine_ref, other_ref, attended_ref, out_ref):
    attended = jnp.sum(parts_ref[...].astype(F32), axis=0).astype(BF16)
    attended_ref[...] = attended
    own = own_half((ROWS_TP, FEAT), 0)
    tokens = jnp.where(own, mine_ref[:ROWS_TP], swap_halves(other_ref[:ROWS_TP]))
    gain = jnp.where(own, mine_ref[ROWS_TP:], other_ref[ROWS_TP:])
    mid = tokens + attended.astype(F32)
    lane = iota((ROWS_TP, 512 - FEAT), 1)
    extra = jnp.zeros(lane.shape, F32)
    for at, part in enumerate(parts_of(jnp.sum(mid * mid, axis=1, keepdims=True))):
        extra = jnp.where(lane == at, part, extra)
    row_data = jnp.concatenate([mid * gain, extra], axis=1).astype(BF16)
    for place in range(N_TP):
        out_ref[place] = row_data


def gate_kernel(rows_ref, own_gate_ref, own_up_ref, other_gate_ref, other_up_ref, out_ref):
    rows = rows_ref[...].astype(F32).reshape(TOKROWS, 512).astype(BF16)
    shape = (CLASS, TOKROWS)
    place, row = iota(shape, 0), iota(shape, 1)
    match = place == row // ROWS_TP * (ROWS_TP // 2) + row % (ROWS_TP // 2)
    own = dot((match & own_half(shape, 1)).astype(F32).astype(BF16), rows).astype(BF16)
    other = dot((match & ~own_half(shape, 1)).astype(F32).astype(BF16), rows).astype(BF16)
    sixteen, column = iota((16, 512), 0), iota((16, 512), 1)
    first = ((sixteen < 3) & (column == FEAT + sixteen)).astype(F32).astype(BF16)
    second = ((sixteen >= 3) & (sixteen < 6) & (column == FEAT + sixteen - 3)).astype(F32).astype(BF16)
    squares = (dot(first, own, NT) + dot(second, other, NT)).astype(BF16)
    own, other = own[:, :FEAT], other[:, :FEAT]
    for place in range(CHIPS):
        columns = slice(place * HID_Y, (place + 1) * HID_Y)
        gate = dot(own, own_gate_ref[0, :, columns]) + dot(other, other_gate_ref[0, :, columns])
        up = dot(own, own_up_ref[0, :, columns]) + dot(other, other_up_ref[0, :, columns])
        out_ref[place, :CLASS, :] = gate.astype(BF16)
        out_ref[place, CLASS : 2 * CLASS, :] = up.astype(BF16)
        out_ref[place, 2 * CLASS :, :] = squares


def hidden_kernel(parts_ref, out_ref):
    gate = jnp.sum(parts_ref[:, :CLASS, :].astype(F32), axis=0)
    up = jnp.sum(parts_ref[:, CLASS : 2 * CLASS, :].astype(F32), axis=0)
    squares = jnp.sum(parts_ref[:, 2 * CLASS :, :].astype(F32), axis=0)
    squares = jnp.sum(squares[:6], axis=0, keepdims=True)
    diagonal = iota((CLASS, CLASS), 0) == iota((CLASS, CLASS), 1)
    squares = jnp.sum(jnp.where(diagonal, squares, 0.0), axis=1, keepdims=True)
    scale = lax.rsqrt(squares / D + EPS)
    gate = gate * scale
    hidden = (gate / (1.0 + jnp.exp(-gate)) * (up * scale)).astype(BF16)
    for place in range(N_KV):
        out_ref[place] = hidden


def down_kernel(hidden_ref, down_ref, out_ref):
    out = jnp.zeros((TOKROWS, FEAT), F32)
    shape = (TOKROWS, CLASS)
    row, source = iota(shape, 0), iota(shape, 1)
    match = source == row // ROWS_TP * (ROWS_TP // 2) + row % (ROWS_TP // 2)
    for core in range(2):
        hidden = jnp.concatenate([hidden_ref[2 * chip + core] for chip in range(CHIPS)], axis=1)
        produced = dot(hidden, down_ref[0], NT).astype(BF16)
        back = (match & (row % ROWS_TP // (ROWS_TP // 2) == core)).astype(F32).astype(BF16)
        out = out + dot(back, produced)
    out_ref[...] = out.reshape(N_TP, ROWS_TP, FEAT).astype(BF16)


def mix_kernel(parts_ref, mine_ref, own_ref, other_ref, ids_ref, weights_ref, attended_ref, out_ref):
    own = own_ref[...].astype(F32)
    attended = jnp.where(own_half(own.shape, 0), own, swap_halves(other_ref[...].astype(F32)))
    attended_ref[...] = attended.astype(BF16)
    total = mine_ref[:ROWS_TP] + attended
    ids = ids_ref[...]
    weights = weights_ref[...]
    for expert in range(EXPERTS):
        share = jnp.sum(jnp.where(ids == expert, weights, 0.0), axis=1, keepdims=True)
        both = parts_ref[2 * expert].astype(F32) + parts_ref[2 * expert + 1].astype(F32)
        total = total + share * both
    out_ref[...] = total.astype(BF16)


def run(kernel, outs, *operands, scratch=(), cost=None, limit=40, after=()):
    single = not isinstance(outs, list)
    placed = [pl.BlockSpec(memory_space=pltpu.VMEM)] * (1 if single else len(outs))
    count = len(operands)

    def body(*refs):
        kernel(*refs[:count], *refs[count + len(after) :])

    return pl.pallas_call(
        body,
        out_shape=outs if single else tuple(outs),
        in_specs=[pl.BlockSpec(memory_space=pltpu.VMEM)] * count + [pl.BlockSpec(memory_space=pl.ANY)] * len(after),
        out_specs=placed[0] if single else tuple(placed),
        scratch_shapes=list(scratch),
        cost_estimate=cost,
        compiler_params=pltpu.CompilerParams(vmem_limit_bytes=limit * 2**20),
    )(*operands, *after)


def shaped(*shape, dtype=BF16):
    return jax.ShapeDtypeStruct(shape, dtype)


def start(tokens, attn_gain, down_kv, key_up, value_up, mlp_gain):
    return run(
        start_kernel, [shaped(CHIPS, UP_ROWS + FRESH_ROWS, 128), shaped(16, FEAT, dtype=F32)],
        tokens, attn_gain.reshape(1, FEAT), down_kv, jnp.swapaxes(key_up, 1, 2), value_up,
        mlp_gain.reshape(1, FEAT), limit=60,
    )


def own_sum(ups):
    return run(sum_kernel, shaped(FRESH_ROWS, 128, dtype=F32), ups)


def fresh(own, other, latent_gain, lengths, after):
    freq = 10000.0 ** (-2.0 * jnp.arange(ROPE // 2, dtype=F32) / ROPE)
    return run(
        fresh_kernel, shaped(N_TP, ROWS_TP, KEY_W),
        own, other, latent_gain.reshape(1, LAT), lengths.reshape(1, SEQS), freq[None], after=after,
    )


def attend(lengths, own, other, query_nope, query_rope, cache):
    return run(
        attend_kernel,
        [
            shaped(TOKROWS, ATT_W),
            shaped(HEADS_DEV * ROWS_KV, KEY),
            shaped(2 * HEADS_DEV, N_KV, LAT_KV, 128),
        ],
        lengths.reshape(1, SEQS), own, other, query_nope, query_rope, jnp.swapaxes(cache, 1, 2),
        scratch=[pltpu.VMEM((SEQS, HEADS_DEV * TOKROWS // SEQS, KEY), BF16)],
        cost=pl.CostEstimate(flops=2_200_000_000, bytes_accessed=4_000_000, transcendentals=800_000),
    )


def merge(parts, own, ups, keys, after):
    return run(merge_kernel, shaped(TOKROWS, ATT_W), parts, own, ups, keys, after=after)


def combine(parts):
    return run(combine_kernel, shaped(CHIPS, ROWS_KV, HEADS_DEV * VDIM), parts)


def project(values, own, other):
    return run(project_kernel, shaped(N_TP, ROWS_TP, FEAT), values, own, other)


def route(parts, mine, other):
    return run(route_kernel, [shaped(ROWS_TP, FEAT), shaped(N_TP, ROWS_TP, 512)], parts, mine, other)


def gate(rows, own_gate, own_up, other_gate, other_up):
    return run(gate_kernel, shaped(CHIPS, PART_ROWS, 128), rows, own_gate, own_up, other_gate, other_up)


def hidden(parts):
    return run(hidden_kernel, shaped(N_KV, CLASS, HID_Y), parts)


def down(packed, down_proj):
    return run(down_kernel, shaped(N_TP, ROWS_TP, FEAT), packed, jnp.swapaxes(down_proj, 1, 2))


def mix(parts, mine, own, other, expert_ids, expert_weights):
    outs = [shaped(ROWS_TP, FEAT), shaped(ROWS_TP, FEAT)]
    return run(mix_kernel, outs, parts, mine, own, other, expert_ids, expert_weights)


def exchange(array, axis, groups=None):
    return lax.all_to_all(array, axis, split_axis=0, concat_axis=0, axis_index_groups=groups, tiled=True)


def along_y(array):
    return exchange(array, "kv", [[2 * chip + core for chip in range(CHIPS)] for core in range(2)])


def other_core(array):
    return lax.ppermute(array, "kv", [(index, index ^ 1) for index in range(N_KV)])


def per_device(
    tokens, attn_gain, down_kv, latent_gain, query_nope, query_rope, cache, lengths, key_up, value_up,
    out_proj, mlp_gain, expert_ids, expert_weights, gate_proj, up_proj, down_proj,
):
    ups, mine = start(tokens, attn_gain, down_kv, key_up, value_up, mlp_gain)
    out_own = out_proj.T
    ups, *moved = lax.optimization_barrier((ups, mine, out_own, gate_proj, up_proj))
    own = along_y(ups)
    moved = [other_core(array) for array in moved]
    part = own_sum(own)
    keys = fresh(part, other_core(part), latent_gain, lengths, moved[2:])
    keys, own = lax.optimization_barrier((keys, own))
    keys = exchange(keys, "tp")
    parts, queries, ups = attend(lengths, own, other_core(own), query_nope, query_rope, cache)
    parts = merge(parts, queries, ups, keys, moved[:2])
    parts = exchange(parts.reshape(N_KV, ROWS_KV, ATT_W), "kv")
    values = along_y(combine(parts))
    parts = exchange(project(values, out_own, moved[1]), "tp")
    attended, rows = route(parts, mine, moved[0])
    other_attended = other_core(attended)
    rows = exchange(rows, "tp")
    parts = along_y(gate(rows, gate_proj, up_proj, moved[2], moved[3]))
    packed = exchange(hidden(parts), "kv")
    parts = exchange(down(packed, down_proj), "tp")
    return mix(parts, mine, attended, other_attended, expert_ids, expert_weights)


def solution(mesh):
    return jax.shard_map(
        per_device,
        mesh=mesh,
        in_specs=(
            P("tp", "kv"),
            P("kv"),
            P("kv", None),
            P(),
            P(None, "tp"),
            P(None, "tp"),
            P(None, "kv", None),
            P(),
            P("tp", None, "kv"),
            P("tp", "kv", None),
            P("tp", "kv"),
            P("kv"),
            P("tp", None),
            P("tp", None),
            P("tp", "kv", None),
            P("tp", "kv", None),
            P("tp", None, "kv"),
        ),
        out_specs=(P("tp", "kv"), P("tp", "kv")),
        check_vma=False,
    )
```

```python
import functools
import math

import jax
import jax.numpy as jnp
from jax import lax
from jax.experimental import pallas as pl
from jax.experimental.pallas import tpu as pltpu
from jax.sharding import PartitionSpec as P

D = 7168
NOPE = 128
ROPE = 64
LAT = 512
VDIM = 128
SEQS = 2
QROWS = 32
STEPS = 4
TOKROWS = 256
EXPERTS = 16

N_KV = 16
N_TP = 32
HEADS_DEV = 4
FEAT = D // N_KV
ROWS_TP = TOKROWS // N_TP
ROWS_KV = TOKROWS // N_KV
KEY = LAT + ROPE
PAIRS = SEQS * QROWS
STAT = 2 * HEADS_DEV
ATT_W = LAT + 128
CHIPS = N_KV // 2
LAT_KV = LAT // N_KV
UP_ROWS = 2 * HEADS_DEV * LAT_KV
FRESH_W = KEY + ROPE
FRESH_ROWS = 48
CLASS = TOKROWS // 2
PART_ROWS = 2 * CLASS + 16
KEY_W = 384
HID = 1024
HID_Y = HID // 8

EPS = 1e-06
LOWEST = -1e30
SCALE = 1.0 / math.sqrt(NOPE + ROPE)

F32 = jnp.float32
BF16 = jnp.bfloat16
NT = (((1,), (1,)), ((), ()))
TN = (((0,), (0,)), ((), ()))


def kv_index():
    return lax.axis_index("kv")


def tp_index():
    return lax.axis_index("tp")


def iota(shape, dim):
    return lax.broadcasted_iota(jnp.int32, shape, dim)


def dot(a, b, dims=(((1,), (0,)), ((), ()))):
    return lax.dot_general(a, b, dims, preferred_element_type=F32)


def parts_of(value):
    high = value.astype(BF16).astype(F32)
    rest = value - high
    middle = rest.astype(BF16).astype(F32)
    return high, middle, rest - middle


def with_stats(stats, head, peak, total):
    lane = iota(stats.shape, 1)
    for at, part in enumerate(parts_of(peak)):
        stats = jnp.where(lane == at * STAT + head, part, stats)
    for at, part in enumerate(parts_of(total)):
        stats = jnp.where(lane == at * STAT + HEADS_DEV + head, part, stats)
    return stats


def whole_stats(tail):
    return tail[..., :STAT] + tail[..., STAT : 2 * STAT] + tail[..., 2 * STAT : 3 * STAT]


def swap_halves(rows):
    return pltpu.roll(rows, 4, 0)


def start_kernel(tokens_ref, gain_ref, down_ref, key_ref, value_ref, mlp_gain_ref, out_ref, mine_ref):
    wide_tokens = tokens_ref[...].astype(F32)
    mine_ref[...] = jnp.concatenate([wide_tokens, jnp.broadcast_to(mlp_gain_ref[...], (8, FEAT))], axis=0)
    normed = (wide_tokens * gain_ref[...]).astype(BF16)
    fresh = dot(normed, down_ref[...])
    fresh = jnp.concatenate([fresh, jnp.zeros((ROWS_TP, ROPE), F32)], axis=1)
    tiles = [fresh[:, at * 128 : (at + 1) * 128] for at in range(FRESH_W // 128)]
    tiles.append(jnp.zeros((FRESH_ROWS - ROWS_TP * len(tiles), 128), F32))
    packed = jnp.concatenate(tiles, axis=0).astype(BF16)
    for place in range(CHIPS):
        for head in range(HEADS_DEV):
            out_ref[place, head * LAT_KV : (head + 1) * LAT_KV, :] = key_ref[head]
            out_ref[place, UP_ROWS // 2 + head * LAT_KV : UP_ROWS // 2 + (head + 1) * LAT_KV, :] = value_ref[head]
        out_ref[place, UP_ROWS:, :] = packed


def sum_kernel(ups_ref, out_ref):
    out_ref[...] = jnp.sum(ups_ref[:, UP_ROWS:, :].astype(F32), axis=0)


def fresh_kernel(own_ref, other_ref, gain_ref, lengths_ref, freq_ref, out_ref):
    packed = own_ref[...] + other_ref[...]
    tiles = [packed[at * ROWS_TP : (at + 1) * ROWS_TP] for at in range(FRESH_W // 128)]
    fresh = jnp.concatenate(tiles[:-1], axis=1)
    turn = tiles[-1][:, :ROPE]
    scaled = fresh * lax.rsqrt(jnp.mean(fresh * fresh, axis=1, keepdims=True) + EPS) * gain_ref[...]
    row = tp_index() * ROWS_TP
    lengths = lengths_ref[...]
    start = jnp.where(row // QROWS % SEQS == 0, lengths[:, 0:1], lengths[:, 1:2])
    angle = (start + row // PAIRS).astype(F32) * freq_ref[...]
    cosine, sine = jnp.cos(angle), jnp.sin(angle)
    first, second = turn[:, : ROPE // 2], turn[:, ROPE // 2 :]
    turned = [first * cosine - second * sine, second * cosine + first * sine]
    key = jnp.concatenate([scaled] + turned + [jnp.zeros((ROWS_TP, ROPE), F32)], axis=1)
    key = jnp.where(kv_index() % 2 == 0, key, swap_halves(key))
    upper = jnp.concatenate([key[:, :256], key[:, LAT:]], axis=1)
    lower = jnp.concatenate([swap_halves(key[:, 256:LAT]), jnp.zeros((ROWS_TP, KEY_W - 256), F32)], axis=1)
    key = jnp.where(iota(upper.shape, 0) < ROWS_TP // 2, upper, lower).astype(BF16)
    for place in range(N_TP):
        out_ref[place] = key


def attend_kernel(
    lengths_ref, own_ups_hbm, other_ups_hbm, nope_hbm, rope_hbm, keys_hbm, other_keys_hbm,
    out_ref, own_ref, ups_ref, queries, nope_ref, rope_ref, keys_ref, other_keys_ref, sems,
):
    kv = kv_index()
    core = kv % 2
    waits = []

    def fetch(source, target):
        waits.append(pltpu.make_async_copy(source, target, sems.at[len(waits)]))
        waits[-1].start()

    fetch(nope_hbm, nope_ref)
    fetch(rope_hbm, rope_ref)
    for which in range(2 * HEADS_DEV):
        rows = pl.ds(which * LAT_KV, LAT_KV)
        fetch(own_ups_hbm.at[:, rows, :], ups_ref.at[which, :, core])
        fetch(other_ups_hbm.at[:, rows, :], ups_ref.at[which, :, 1 - core])
    fetch(keys_hbm, keys_ref)
    fetch(other_keys_hbm, other_keys_ref)
    row, source = iota((CLASS, TOKROWS), 0), iota((CLASS, TOKROWS), 1)
    pair = row // ROWS_KV * ROWS_TP + core * (ROWS_TP // 2) + row % ROWS_KV // STEPS
    reorder = (source == row % STEPS * PAIRS + pair).astype(F32).astype(BF16)
    rows_seq = CLASS // SEQS
    for wait in waits[:-2]:
        wait.wait()
    nope = dot(reorder, nope_ref[...]).astype(BF16)
    rope = dot(reorder, rope_ref[...]).astype(BF16)
    for head in range(HEADS_DEV):
        key_up = ups_ref[head].reshape(LAT, NOPE)
        absorbed = dot(nope[:, head * NOPE : (head + 1) * NOPE], key_up, NT).astype(BF16)
        turned = rope[:, head * ROPE : (head + 1) * ROPE]
        for seq in range(SEQS):
            rows = slice(seq * rows_seq, (seq + 1) * rows_seq)
            place = slice(head * rows_seq, (head + 1) * rows_seq)
            queries[seq, place, :LAT] = absorbed[rows]
            queries[seq, place, LAT:] = turned[rows]
    own_seq = kv // (N_KV // SEQS)
    own_row = kv // 2 % (CHIPS // SEQS) * ROWS_KV
    for head in range(HEADS_DEV):
        begin = pl.multiple_of(head * rows_seq + own_row, ROWS_KV)
        own_ref[head * ROWS_KV : (head + 1) * ROWS_KV, :] = queries[own_seq, pl.ds(begin, ROWS_KV), :]
    for wait in waits[-2:]:
        wait.wait()
    span = keys_ref.shape[2]
    lengths = lengths_ref[...]
    for seq in range(SEQS):
        blocks = []
        for keys, index in ((keys_ref, kv), (other_keys_ref, kv + 1 - 2 * core)):
            valid = index * span + iota((1, span), 1) < lengths[:, seq : seq + 1]
            scores = dot(queries[seq], keys[seq]) * SCALE + jnp.where(valid, 0.0, LOWEST)
            blocks.append((keys, valid, scores, jnp.max(scores, axis=1, keepdims=True)))
        peak = jnp.maximum(blocks[0][3], blocks[1][3])
        total, latent = 0.0, 0.0
        for keys, valid, scores, _ in blocks:
            weights = jnp.where(valid, jnp.exp(scores - peak), 0.0).astype(BF16)
            total = total + jnp.sum(weights.astype(F32), axis=1, keepdims=True)
            latent = latent + dot(weights, keys[seq, :LAT, :], NT)
        latent = latent.astype(BF16)
        stats = jnp.zeros((rows_seq, 128), F32)
        rows = slice(seq * rows_seq, (seq + 1) * rows_seq)
        for head in range(HEADS_DEV):
            place = slice(head * rows_seq, (head + 1) * rows_seq)
            value_up = ups_ref[HEADS_DEV + head].reshape(LAT, VDIM)
            out_ref[rows, head * VDIM : (head + 1) * VDIM] = dot(latent[place], value_up).astype(BF16)
            stats = with_stats(stats, head, peak[place], total[place])
        out_ref[rows, LAT:] = stats.astype(BF16)


def merge_kernel(parts_ref, own_ref, ups_ref, keys_ref, out_ref):
    kv = kv_index()
    out_ref[...] = parts_ref[...]
    rows = pl.ds(pl.multiple_of(kv // 2 * ROWS_KV, ROWS_KV), ROWS_KV)
    mine = parts_ref[rows, :].astype(F32)
    stats = whole_stats(mine[:, LAT:])
    keys = []
    for step in range(STEPS):
        block = keys_ref[step * (PAIRS // ROWS_TP) + kv // 2].astype(F32)
        keys.append(jnp.concatenate([block[:, :256], swap_halves(block[:, :256]), block[:, 256 : 256 + ROPE]], axis=1))
    keys = jnp.concatenate(keys, axis=0).astype(BF16)
    scores = dot(own_ref[...], keys, NT) * SCALE
    row = iota(scores.shape, 0) % ROWS_KV
    key = iota(scores.shape, 1)
    causal = (row // STEPS == key % ROWS_TP) & (key // ROWS_TP <= row % STEPS)
    scores = jnp.where(causal, scores, LOWEST)
    fresh_peak = jnp.max(scores, axis=1, keepdims=True)
    weights = jnp.where(causal, jnp.exp(scores - fresh_peak), 0.0).astype(BF16)
    fresh_total = jnp.sum(weights.astype(F32), axis=1, keepdims=True)
    fresh_latent = dot(weights, keys[:, :LAT]).astype(BF16)
    tail = jnp.zeros((ROWS_KV, 128), F32)
    merged = []
    for head in range(HEADS_DEV):
        own = slice(head * ROWS_KV, (head + 1) * ROWS_KV)
        peak = stats[:, head : head + 1]
        top = jnp.maximum(peak, fresh_peak[own])
        keep = jnp.exp(peak - top)
        fresh_keep = jnp.exp(fresh_peak[own] - top)
        value_up = ups_ref[HEADS_DEV + head].reshape(LAT, VDIM)
        part = mine[:, head * VDIM : (head + 1) * VDIM]
        merged.append(part * keep + dot(fresh_latent[own], value_up) * fresh_keep)
        total = stats[:, HEADS_DEV + head : HEADS_DEV + head + 1] * keep + fresh_total[own] * fresh_keep
        tail = with_stats(tail, head, top, total)
    out_ref[rows, :] = jnp.concatenate(merged + [tail], axis=1).astype(BF16)


def combine_kernel(parts_ref, out_ref):
    stats = whole_stats(parts_ref[:, :, LAT:].astype(F32))
    for head in range(HEADS_DEV):
        peak = stats[:, :, head : head + 1]
        total = stats[:, :, HEADS_DEV + head : HEADS_DEV + head + 1]
        keep = jnp.exp(peak - jnp.max(peak, axis=0, keepdims=True))
        part = parts_ref[:, :, head * VDIM : (head + 1) * VDIM].astype(F32)
        value = jnp.sum(part * keep, axis=0) / jnp.sum(total * keep, axis=0)
        for place in range(CHIPS):
            out_ref[place, :, head * VDIM : (head + 1) * VDIM] = value.astype(BF16)


def own_half(shape, dim):
    return iota(shape, dim) % ROWS_TP // (ROWS_TP // 2) == kv_index() % 2


def project_kernel(values_ref, own_ref, other_ref, out_ref):
    values = values_ref[...].reshape(CLASS, HEADS_DEV * VDIM)
    shape = (TOKROWS, CLASS)
    row, source = iota(shape, 0), iota(shape, 1)
    block, pair = row // ROWS_TP, row % (ROWS_TP // 2)
    match = source == block % CHIPS * ROWS_KV + pair * STEPS + block // CHIPS
    own = (match & own_half(shape, 0)).astype(F32).astype(BF16)
    other = (match & ~own_half(shape, 0)).astype(F32).astype(BF16)
    out = dot(dot(own, values).astype(BF16), own_ref[...], NT)
    out = out + dot(dot(other, values).astype(BF16), other_ref[...], NT)
    out_ref[...] = out.reshape(N_TP, ROWS_TP, FEAT).astype(BF16)


def route_kernel(parts_ref, mine_ref, other_ref, attended_ref, mid_ref, out_ref):
    attended = jnp.sum(parts_ref[...].astype(F32), axis=0).astype(BF16)
    attended_ref[...] = attended
    own = own_half((ROWS_TP, FEAT), 0)
    tokens = jnp.where(own, mine_ref[:ROWS_TP], swap_halves(other_ref[:ROWS_TP]))
    gain = jnp.where(own, mine_ref[ROWS_TP:], other_ref[ROWS_TP:])
    mid = tokens + attended.astype(F32)
    mid_ref[...] = mid
    lane = iota((ROWS_TP, 512 - FEAT), 1)
    extra = jnp.zeros(lane.shape, F32)
    for at, part in enumerate(parts_of(jnp.sum(mid * mid, axis=1, keepdims=True))):
        extra = jnp.where(lane == at, part, extra)
    row_data = jnp.concatenate([mid * gain, extra], axis=1).astype(BF16)
    for place in range(N_TP):
        out_ref[place] = row_data


def gate_kernel(rows_ref, own_gate_ref, own_up_ref, other_gate_ref, other_up_ref, out_ref):
    rows = rows_ref[...].astype(F32).reshape(TOKROWS, 512).astype(BF16)
    shape = (CLASS, TOKROWS)
    place, row = iota(shape, 0), iota(shape, 1)
    match = place == row // ROWS_TP * (ROWS_TP // 2) + row % (ROWS_TP // 2)
    own = dot((match & own_half(shape, 1)).astype(F32).astype(BF16), rows).astype(BF16)
    other = dot((match & ~own_half(shape, 1)).astype(F32).astype(BF16), rows).astype(BF16)
    sixteen, column = iota((16, 512), 0), iota((16, 512), 1)
    first = ((sixteen < 3) & (column == FEAT + sixteen)).astype(F32).astype(BF16)
    second = ((sixteen >= 3) & (sixteen < 6) & (column == FEAT + sixteen - 3)).astype(F32).astype(BF16)
    squares = (dot(first, own, NT) + dot(second, other, NT)).astype(BF16)
    own, other = own[:, :FEAT], other[:, :FEAT]
    for place in range(CHIPS):
        columns = slice(place * HID_Y, (place + 1) * HID_Y)
        gate = dot(own, own_gate_ref[0, :, columns]) + dot(other, other_gate_ref[0, :, columns])
        up = dot(own, own_up_ref[0, :, columns]) + dot(other, other_up_ref[0, :, columns])
        out_ref[place, :CLASS, :] = gate.astype(BF16)
        out_ref[place, CLASS : 2 * CLASS, :] = up.astype(BF16)
        out_ref[place, 2 * CLASS :, :] = squares


def hidden_kernel(parts_ref, out_ref):
    gate = jnp.sum(parts_ref[:, :CLASS, :].astype(F32), axis=0)
    up = jnp.sum(parts_ref[:, CLASS : 2 * CLASS, :].astype(F32), axis=0)
    squares = jnp.sum(parts_ref[:, 2 * CLASS :, :].astype(F32), axis=0)
    squares = jnp.sum(squares[:6], axis=0, keepdims=True)
    diagonal = iota((CLASS, CLASS), 0) == iota((CLASS, CLASS), 1)
    squares = jnp.sum(jnp.where(diagonal, squares, 0.0), axis=1, keepdims=True)
    scale = lax.rsqrt(squares / D + EPS)
    gate = gate * scale
    hidden = (gate / (1.0 + jnp.exp(-gate)) * (up * scale)).astype(BF16)
    for place in range(CHIPS):
        out_ref[place] = hidden


def down_kernel(hidden_ref, own_ref, other_ref, out_ref):
    hidden = jnp.concatenate([hidden_ref[chip] for chip in range(CHIPS)], axis=1)
    shape = (TOKROWS, CLASS)
    row, source = iota(shape, 0), iota(shape, 1)
    match = source == row // ROWS_TP * (ROWS_TP // 2) + row % (ROWS_TP // 2)
    own = (match & own_half(shape, 0)).astype(F32).astype(BF16)
    other = (match & ~own_half(shape, 0)).astype(F32).astype(BF16)
    out = dot(own, dot(hidden, own_ref[0], NT).astype(BF16))
    out = out + dot(other, dot(hidden, other_ref[0], NT).astype(BF16))
    out_ref[...] = out.reshape(N_TP, ROWS_TP, FEAT).astype(BF16)


def mix_kernel(parts_ref, mid_ref, ids_ref, weights_ref, out_ref):
    ids = ids_ref[...].astype(F32)
    weights = weights_ref[...]
    own = own_half(ids.shape, 0)
    ids = jnp.where(own, ids, swap_halves(ids))
    weights = jnp.where(own, weights, swap_halves(weights))
    total = mid_ref[...]
    for expert in range(EXPERTS):
        share = jnp.sum(jnp.where(ids == float(expert), weights, 0.0), axis=1, keepdims=True)
        both = parts_ref[2 * expert].astype(F32) + parts_ref[2 * expert + 1].astype(F32)
        total = total + share * both
    out_ref[...] = total.astype(BF16)


def finish_kernel(own_attended_ref, other_attended_ref, own_mixed_ref, other_mixed_ref, attended_ref, mixed_ref):
    own = own_half((ROWS_TP, FEAT), 0)
    for mine_ref, other_ref, out_ref in (
        (own_attended_ref, other_attended_ref, attended_ref),
        (own_mixed_ref, other_mixed_ref, mixed_ref),
    ):
        other = swap_halves(other_ref[...].astype(F32))
        out_ref[...] = jnp.where(own, mine_ref[...].astype(F32), other).astype(BF16)


def run(kernel, outs, *operands, fetched=(), scratch=(), cost=None, limit=40, after=()):
    single = not isinstance(outs, list)
    placed = [pl.BlockSpec(memory_space=pltpu.VMEM)] * (1 if single else len(outs))
    count = len(operands) + len(fetched)
    left = len(fetched) + len(after)

    def body(*refs):
        kernel(*refs[:count], *refs[count + len(after) :])

    return pl.pallas_call(
        body,
        out_shape=outs if single else tuple(outs),
        in_specs=[pl.BlockSpec(memory_space=pltpu.VMEM)] * len(operands) + [pl.BlockSpec(memory_space=pl.ANY)] * left,
        out_specs=placed[0] if single else tuple(placed),
        scratch_shapes=list(scratch),
        cost_estimate=cost,
        compiler_params=pltpu.CompilerParams(vmem_limit_bytes=limit * 2**20),
    )(*operands, *fetched, *after)


def shaped(*shape, dtype=BF16):
    return jax.ShapeDtypeStruct(shape, dtype)


def start(tokens, attn_gain, down_kv, key_up, value_up, mlp_gain):
    return run(
        start_kernel, [shaped(CHIPS, UP_ROWS + FRESH_ROWS, 128), shaped(16, FEAT, dtype=F32)],
        tokens, attn_gain.reshape(1, FEAT), down_kv, jnp.swapaxes(key_up, 1, 2), value_up,
        mlp_gain.reshape(1, FEAT), limit=60,
    )


def own_sum(ups, after):
    return run(sum_kernel, shaped(FRESH_ROWS, 128, dtype=F32), ups, after=after)


def fresh(own, other, latent_gain, lengths):
    freq = 10000.0 ** (-2.0 * jnp.arange(ROPE // 2, dtype=F32) / ROPE)
    return run(
        fresh_kernel, shaped(N_TP, ROWS_TP, KEY_W),
        own, other, latent_gain.reshape(1, LAT), lengths.reshape(1, SEQS), freq[None],
    )


def attend(lengths, own, other, query_nope, query_rope, keys, other_keys):
    return run(
        attend_kernel,
        [
            shaped(CLASS, ATT_W),
            shaped(HEADS_DEV * ROWS_KV, KEY),
            shaped(2 * HEADS_DEV, CHIPS, 2, LAT_KV, 128),
        ],
        lengths.reshape(1, SEQS),
        fetched=(own, other, query_nope, query_rope, keys, other_keys),
        scratch=[
            pltpu.VMEM((SEQS, HEADS_DEV * CLASS // SEQS, KEY), BF16),
            pltpu.VMEM(query_nope.shape, BF16),
            pltpu.VMEM(query_rope.shape, BF16),
            pltpu.VMEM(keys.shape, BF16),
            pltpu.VMEM(keys.shape, BF16),
            pltpu.SemaphoreType.DMA((4 + 4 * HEADS_DEV,)),
        ],
        cost=pl.CostEstimate(flops=2_200_000_000, bytes_accessed=4_000_000, transcendentals=800_000),
        limit=20,
    )


def merge(parts, own, ups, keys):
    return run(merge_kernel, shaped(CLASS, ATT_W), parts, own, ups, keys)


def combine(parts):
    return run(combine_kernel, shaped(CHIPS, ROWS_KV, HEADS_DEV * VDIM), parts)


def project(values, own, other):
    return run(project_kernel, shaped(N_TP, ROWS_TP, FEAT), values, own, other)


def route(parts, mine, other):
    outs = [shaped(ROWS_TP, FEAT), shaped(ROWS_TP, FEAT, dtype=F32), shaped(N_TP, ROWS_TP, 512)]
    return run(route_kernel, outs, parts, mine, other)


def gate(rows, own_gate, own_up, other_gate, other_up):
    return run(gate_kernel, shaped(CHIPS, PART_ROWS, 128), rows, own_gate, own_up, other_gate, other_up)


def hidden(parts):
    return run(hidden_kernel, shaped(CHIPS, CLASS, HID_Y), parts)


def down(packed, own, other):
    return run(down_kernel, shaped(N_TP, ROWS_TP, FEAT), packed, own, other)


def mix(parts, mid, expert_ids, expert_weights):
    return run(mix_kernel, shaped(ROWS_TP, FEAT), parts, mid, expert_ids, expert_weights)


def finish(own_attended, other_attended, own_mixed, other_mixed):
    outs = [shaped(ROWS_TP, FEAT), shaped(ROWS_TP, FEAT)]
    return run(finish_kernel, outs, own_attended, other_attended, own_mixed, other_mixed)


def exchange(array, axis, groups=None):
    return lax.all_to_all(array, axis, split_axis=0, concat_axis=0, axis_index_groups=groups, tiled=True)


def along_y(array):
    return exchange(array, "kv", [[2 * chip + core for chip in range(CHIPS)] for core in range(2)])


def other_core(array):
    return lax.ppermute(array, "kv", [(index, index ^ 1) for index in range(N_KV)])


def per_device(
    tokens, attn_gain, down_kv, latent_gain, query_nope, query_rope, cache, lengths, key_up, value_up,
    out_proj, mlp_gain, expert_ids, expert_weights, gate_proj, up_proj, down_proj,
):
    ups, mine = start(tokens, attn_gain, down_kv, key_up, value_up, mlp_gain)
    own_cache, own_out, own_down = jnp.swapaxes(cache, 1, 2), out_proj.T, jnp.swapaxes(down_proj, 1, 2)
    ups, *moved = lax.optimization_barrier((ups, own_cache, mine, own_out, gate_proj, up_proj, own_down))
    own = along_y(ups)
    moved = [other_core(array) for array in moved]
    other_cache, other_mine, other_out, other_gate, other_up, other_down = moved
    part = own_sum(own, moved)
    keys = fresh(part, other_core(part), latent_gain, lengths)
    keys, own = lax.optimization_barrier((keys, own))
    keys = exchange(keys, "tp")
    parts, queries, ups = attend(lengths, own, other_core(own), query_nope, query_rope, own_cache, other_cache)
    parts = merge(parts, queries, ups, keys)
    parts = along_y(parts.reshape(CHIPS, ROWS_KV, ATT_W))
    values = along_y(combine(parts))
    parts = exchange(project(values, own_out, other_out), "tp")
    attended, mid, rows = route(parts, mine, other_mine)
    other_attended = other_core(attended)
    rows = exchange(rows, "tp")
    parts = along_y(gate(rows, gate_proj, up_proj, other_gate, other_up))
    packed = along_y(hidden(parts))
    parts = exchange(down(packed, own_down, other_down), "tp")
    mixed = mix(parts, mid, expert_ids, expert_weights)
    return finish(attended, other_attended, mixed, other_core(mixed))


def solution(mesh):
    return jax.shard_map(
        per_device,
        mesh=mesh,
        in_specs=(
            P("tp", "kv"),
            P("kv"),
            P("kv", None),
            P(),
            P(None, "tp"),
            P(None, "tp"),
            P(None, "kv", None),
            P(),
            P("tp", None, "kv"),
            P("tp", "kv", None),
            P("tp", "kv"),
            P("kv"),
            P("tp", None),
            P("tp", None),
            P("tp", "kv", None),
            P("tp", "kv", None),
            P("tp", None, "kv"),
        ),
        out_specs=(P("tp", "kv"), P("tp", "kv")),
        check_vma=False,
    )
```

```python
import functools
import math

import jax
import jax.numpy as jnp
from jax import lax
from jax.experimental import pallas as pl
from jax.experimental.pallas import tpu as pltpu
from jax.sharding import PartitionSpec as P

D = 7168
NOPE = 128
ROPE = 64
LAT = 512
VDIM = 128
SEQS = 2
QROWS = 32
STEPS = 4
TOKROWS = 256
EXPERTS = 16

N_KV = 16
N_TP = 32
HEADS_DEV = 4
FEAT = D // N_KV
ROWS_TP = TOKROWS // N_TP
ROWS_KV = TOKROWS // N_KV
KEY = LAT + ROPE
PAIRS = SEQS * QROWS
STAT = 2 * HEADS_DEV
ATT_W = LAT + 128
CHIPS = N_KV // 2
LAT_KV = LAT // N_KV
UP_ROWS = 2 * HEADS_DEV * LAT_KV
FRESH_W = KEY + ROPE
FRESH_ROWS = 48
TOKEN_AT = FRESH_ROWS
GAIN_AT = TOKEN_AT + 4 * ROWS_TP
PACK_ROWS = GAIN_AT + 4 * ROWS_TP
CLASS = TOKROWS // 2
PART_ROWS = 2 * CLASS + 16
KEY_W = 384
HID = 1024
HID_Y = HID // 8

EPS = 1e-06
LOWEST = -1e30
SCALE = 1.0 / math.sqrt(NOPE + ROPE)

F32 = jnp.float32
BF16 = jnp.bfloat16
NT = (((1,), (1,)), ((), ()))
TN = (((0,), (0,)), ((), ()))


def kv_index():
    return lax.axis_index("kv")


def tp_index():
    return lax.axis_index("tp")


def iota(shape, dim):
    return lax.broadcasted_iota(jnp.int32, shape, dim)


def dot(a, b, dims=(((1,), (0,)), ((), ()))):
    return lax.dot_general(a, b, dims, preferred_element_type=F32)


def parts_of(value):
    high = value.astype(BF16).astype(F32)
    rest = value - high
    middle = rest.astype(BF16).astype(F32)
    return high, middle, rest - middle


def with_stats(stats, head, peak, total):
    lane = iota(stats.shape, 1)
    for at, part in enumerate(parts_of(peak)):
        stats = jnp.where(lane == at * STAT + head, part, stats)
    for at, part in enumerate(parts_of(total)):
        stats = jnp.where(lane == at * STAT + HEADS_DEV + head, part, stats)
    return stats


def whole_stats(tail):
    return tail[..., :STAT] + tail[..., STAT : 2 * STAT] + tail[..., 2 * STAT : 3 * STAT]


def swap_halves(rows):
    return pltpu.roll(rows, 4, 0)


def in_tiles(rows):
    rows = jnp.concatenate([rows, jnp.zeros((ROWS_TP, 512 - FEAT), F32)], axis=1)
    return [rows[:, at * 128 : (at + 1) * 128] for at in range(4)]


def from_tiles(tiles):
    return jnp.concatenate([tiles[at * ROWS_TP : (at + 1) * ROWS_TP] for at in range(4)], axis=1)[:, :FEAT]


def start_kernel(tokens_ref, gain_ref, down_ref, key_ref, value_ref, mlp_gain_ref, out_ref, mine_ref):
    wide_tokens = tokens_ref[...].astype(F32)
    mine_ref[...] = jnp.concatenate(
        in_tiles(wide_tokens) + in_tiles(jnp.broadcast_to(mlp_gain_ref[...], (ROWS_TP, FEAT))), axis=0
    )
    normed = (wide_tokens * gain_ref[...]).astype(BF16)
    fresh = dot(normed, down_ref[...])
    fresh = jnp.concatenate([fresh, jnp.zeros((ROWS_TP, ROPE), F32)], axis=1)
    tiles = [fresh[:, at * 128 : (at + 1) * 128] for at in range(FRESH_W // 128)]
    tiles.append(jnp.zeros((FRESH_ROWS - ROWS_TP * len(tiles), 128), F32))
    packed = jnp.concatenate(tiles, axis=0).astype(BF16)
    for place in range(CHIPS):
        for head in range(HEADS_DEV):
            out_ref[place, head * LAT_KV : (head + 1) * LAT_KV, :] = key_ref[head]
            out_ref[place, UP_ROWS // 2 + head * LAT_KV : UP_ROWS // 2 + (head + 1) * LAT_KV, :] = value_ref[head]
        out_ref[place, UP_ROWS:, :] = packed


def sum_kernel(ups_hbm, mine_hbm, out_ref, fresh_ref, mine_ref, sems):
    fetches = [
        pltpu.make_async_copy(ups_hbm.at[:, pl.ds(UP_ROWS, FRESH_ROWS), :], fresh_ref, sems.at[0]),
        pltpu.make_async_copy(mine_hbm, mine_ref, sems.at[1]),
    ]
    for fetch in fetches:
        fetch.start()
    for fetch in fetches:
        fetch.wait()
    out_ref[FRESH_ROWS:, :] = mine_ref[...]
    out_ref[:FRESH_ROWS, :] = jnp.sum(fresh_ref[...].astype(F32), axis=0)


def fresh_kernel(own_ref, other_ref, gain_ref, lengths_ref, freq_ref, out_hbm, out_ref, sem):
    packed = own_ref[:FRESH_ROWS, :] + other_ref[:FRESH_ROWS, :]
    tiles = [packed[at * ROWS_TP : (at + 1) * ROWS_TP] for at in range(FRESH_W // 128)]
    fresh = jnp.concatenate(tiles[:-1], axis=1)
    turn = tiles[-1][:, :ROPE]
    scaled = fresh * lax.rsqrt(jnp.mean(fresh * fresh, axis=1, keepdims=True) + EPS) * gain_ref[...]
    row = tp_index() * ROWS_TP
    lengths = lengths_ref[...]
    start = jnp.where(row // QROWS % SEQS == 0, lengths[:, 0:1], lengths[:, 1:2])
    angle = (start + row // PAIRS).astype(F32) * freq_ref[...]
    cosine, sine = jnp.cos(angle), jnp.sin(angle)
    first, second = turn[:, : ROPE // 2], turn[:, ROPE // 2 :]
    turned = [first * cosine - second * sine, second * cosine + first * sine]
    key = jnp.concatenate([scaled] + turned + [jnp.zeros((ROWS_TP, ROPE), F32)], axis=1)
    key = jnp.where(kv_index() % 2 == 0, key, swap_halves(key))
    upper = jnp.concatenate([key[:, :256], key[:, LAT:]], axis=1)
    lower = jnp.concatenate([swap_halves(key[:, 256:LAT]), jnp.zeros((ROWS_TP, KEY_W - 256), F32)], axis=1)
    key = jnp.where(iota(upper.shape, 0) < ROWS_TP // 2, upper, lower).astype(BF16)
    for place in range(N_TP):
        out_ref[place] = key
    leave = pltpu.make_async_copy(out_ref, out_hbm, sem)
    leave.start()
    leave.wait()


def attend_kernel(
    lengths_ref, own_ups_hbm, other_ups_hbm, nope_hbm, rope_hbm, keys_hbm, other_keys_hbm,
    out_ref, own_hbm, values_hbm, ups_ref, own_ref, queries, nope_ref, rope_ref, keys_ref, other_keys_ref, sems,
):
    kv = kv_index()
    core = kv % 2
    waits = []

    def fetch(source, target):
        waits.append(pltpu.make_async_copy(source, target, sems.at[len(waits)]))
        waits[-1].start()

    fetch(nope_hbm, nope_ref)
    fetch(rope_hbm, rope_ref)
    for which in range(2 * HEADS_DEV):
        rows = pl.ds(which * LAT_KV, LAT_KV)
        fetch(own_ups_hbm.at[:, rows, :], ups_ref.at[which, :, core])
        fetch(other_ups_hbm.at[:, rows, :], ups_ref.at[which, :, 1 - core])
    fetch(keys_hbm, keys_ref)
    fetch(other_keys_hbm, other_keys_ref)
    row, source = iota((CLASS, TOKROWS), 0), iota((CLASS, TOKROWS), 1)
    pair = row // ROWS_KV * ROWS_TP + core * (ROWS_TP // 2) + row % ROWS_KV // STEPS
    reorder = (source == row % STEPS * PAIRS + pair).astype(F32).astype(BF16)
    rows_seq = CLASS // SEQS
    for wait in waits[:-2]:
        wait.wait()
    nope = dot(reorder, nope_ref[...]).astype(BF16)
    rope = dot(reorder, rope_ref[...]).astype(BF16)
    for head in range(HEADS_DEV):
        key_up = ups_ref[head].reshape(LAT, NOPE)
        absorbed = dot(nope[:, head * NOPE : (head + 1) * NOPE], key_up, NT).astype(BF16)
        turned = rope[:, head * ROPE : (head + 1) * ROPE]
        for seq in range(SEQS):
            rows = slice(seq * rows_seq, (seq + 1) * rows_seq)
            place = slice(head * rows_seq, (head + 1) * rows_seq)
            queries[seq, place, :LAT] = absorbed[rows]
            queries[seq, place, LAT:] = turned[rows]
    own_seq = kv // (N_KV // SEQS)
    own_row = kv // 2 % (CHIPS // SEQS) * ROWS_KV
    for head in range(HEADS_DEV):
        begin = pl.multiple_of(head * rows_seq + own_row, ROWS_KV)
        own_ref[head * ROWS_KV : (head + 1) * ROWS_KV, :] = queries[own_seq, pl.ds(begin, ROWS_KV), :]
    leaves = [
        pltpu.make_async_copy(own_ref, own_hbm, sems.at[len(waits)]),
        pltpu.make_async_copy(ups_ref.at[pl.ds(HEADS_DEV, HEADS_DEV)], values_hbm, sems.at[len(waits) + 1]),
    ]
    for leave in leaves:
        leave.start()
    for wait in waits[-2:]:
        wait.wait()
    span = keys_ref.shape[2]
    lengths = lengths_ref[...]
    for seq in range(SEQS):
        blocks = []
        for keys, index in ((keys_ref, kv), (other_keys_ref, kv + 1 - 2 * core)):
            valid = index * span + iota((1, span), 1) < lengths[:, seq : seq + 1]
            scores = dot(queries[seq], keys[seq]) * SCALE + jnp.where(valid, 0.0, LOWEST)
            blocks.append((keys, valid, scores, jnp.max(scores, axis=1, keepdims=True)))
        peak = jnp.maximum(blocks[0][3], blocks[1][3])
        total, latent = 0.0, 0.0
        for keys, valid, scores, _ in blocks:
            weights = jnp.where(valid, jnp.exp(scores - peak), 0.0).astype(BF16)
            total = total + jnp.sum(weights.astype(F32), axis=1, keepdims=True)
            latent = latent + dot(weights, keys[seq, :LAT, :], NT)
        latent = latent.astype(BF16)
        stats = jnp.zeros((rows_seq, 128), F32)
        rows = slice(seq * rows_seq, (seq + 1) * rows_seq)
        for head in range(HEADS_DEV):
            place = slice(head * rows_seq, (head + 1) * rows_seq)
            value_up = ups_ref[HEADS_DEV + head].reshape(LAT, VDIM)
            out_ref[rows, head * VDIM : (head + 1) * VDIM] = dot(latent[place], value_up).astype(BF16)
            stats = with_stats(stats, head, peak[place], total[place])
        out_ref[rows, LAT:] = stats.astype(BF16)
    for leave in leaves:
        leave.wait()


def combine_kernel(parts_ref, keys_ref, own_hbm, values_hbm, out_ref, own_ref, values_ref, sems):
    fetches = [
        pltpu.make_async_copy(own_hbm, own_ref, sems.at[0]),
        pltpu.make_async_copy(values_hbm, values_ref, sems.at[1]),
    ]
    for fetch in fetches:
        fetch.start()
    kv = kv_index()
    stats = whole_stats(parts_ref[:, :, LAT:].astype(F32))
    keys = []
    for step in range(STEPS):
        block = keys_ref[step * (PAIRS // ROWS_TP) + kv // 2].astype(F32)
        keys.append(jnp.concatenate([block[:, :256], swap_halves(block[:, :256]), block[:, 256 : 256 + ROPE]], axis=1))
    keys = jnp.concatenate(keys, axis=0).astype(BF16)
    for fetch in fetches:
        fetch.wait()
    scores = dot(own_ref[...], keys, NT) * SCALE
    row = iota(scores.shape, 0) % ROWS_KV
    key = iota(scores.shape, 1)
    causal = (row // STEPS == key % ROWS_TP) & (key // ROWS_TP <= row % STEPS)
    scores = jnp.where(causal, scores, LOWEST)
    fresh_peak = jnp.max(scores, axis=1, keepdims=True)
    weights = jnp.where(causal, jnp.exp(scores - fresh_peak), 0.0).astype(BF16)
    fresh_total = jnp.sum(weights.astype(F32), axis=1, keepdims=True)
    fresh_latent = dot(weights, keys[:, :LAT]).astype(BF16)
    for head in range(HEADS_DEV):
        own = slice(head * ROWS_KV, (head + 1) * ROWS_KV)
        peak = stats[:, :, head : head + 1]
        total = stats[:, :, HEADS_DEV + head : HEADS_DEV + head + 1]
        top = jnp.maximum(jnp.max(peak, axis=0), fresh_peak[own])
        keep = jnp.exp(peak - top[None])
        fresh_keep = jnp.exp(fresh_peak[own] - top)
        value_up = values_ref[head].reshape(LAT, VDIM)
        part = parts_ref[:, :, head * VDIM : (head + 1) * VDIM].astype(F32)
        value = jnp.sum(part * keep, axis=0) + dot(fresh_latent[own], value_up) * fresh_keep
        whole = jnp.sum(total * keep, axis=0) + fresh_total[own] * fresh_keep
        value = (value / whole).astype(BF16)
        for place in range(CHIPS):
            out_ref[place, :, head * VDIM : (head + 1) * VDIM] = value


def own_half(shape, dim):
    return iota(shape, dim) % ROWS_TP // (ROWS_TP // 2) == kv_index() % 2


def project_kernel(values_ref, own_ref, other_ref, out_ref):
    values = values_ref[...].reshape(CLASS, HEADS_DEV * VDIM)
    shape = (TOKROWS, CLASS)
    row, source = iota(shape, 0), iota(shape, 1)
    block, pair = row // ROWS_TP, row % (ROWS_TP // 2)
    match = source == block % CHIPS * ROWS_KV + pair * STEPS + block // CHIPS
    own = (match & own_half(shape, 0)).astype(F32).astype(BF16)
    other = (match & ~own_half(shape, 0)).astype(F32).astype(BF16)
    out = dot(dot(own, values).astype(BF16), own_ref[...], NT)
    out = out + dot(dot(other, values).astype(BF16), other_ref[...], NT)
    out_ref[...] = out.reshape(N_TP, ROWS_TP, FEAT).astype(BF16)


def route_kernel(parts_ref, mine_ref, other_ref, attended_ref, out_ref):
    attended = jnp.sum(parts_ref[...].astype(F32), axis=0).astype(BF16)
    attended_ref[...] = attended
    own = own_half((ROWS_TP, FEAT), 0)
    tokens = jnp.where(own, from_tiles(mine_ref[TOKEN_AT:, :]), swap_halves(from_tiles(other_ref[TOKEN_AT:, :])))
    gain = jnp.where(own, from_tiles(mine_ref[GAIN_AT:, :]), from_tiles(other_ref[GAIN_AT:, :]))
    mid = tokens + attended.astype(F32)
    lane = iota((ROWS_TP, 512 - FEAT), 1)
    extra = jnp.zeros(lane.shape, F32)
    for at, part in enumerate(parts_of(jnp.sum(mid * mid, axis=1, keepdims=True))):
        extra = jnp.where(lane == at, part, extra)
    row_data = jnp.concatenate([mid * gain, extra], axis=1).astype(BF16)
    for place in range(N_TP):
        out_ref[place] = row_data


def gate_kernel(rows_ref, own_gate_ref, own_up_ref, other_gate_ref, other_up_ref, out_ref):
    rows = rows_ref[...].astype(F32).reshape(TOKROWS, 512).astype(BF16)
    shape = (CLASS, TOKROWS)
    place, row = iota(shape, 0), iota(shape, 1)
    match = place == row // ROWS_TP * (ROWS_TP // 2) + row % (ROWS_TP // 2)
    own = dot((match & own_half(shape, 1)).astype(F32).astype(BF16), rows).astype(BF16)
    other = dot((match & ~own_half(shape, 1)).astype(F32).astype(BF16), rows).astype(BF16)
    sixteen, column = iota((16, 512), 0), iota((16, 512), 1)
    first = ((sixteen < 3) & (column == FEAT + sixteen)).astype(F32).astype(BF16)
    second = ((sixteen >= 3) & (sixteen < 6) & (column == FEAT + sixteen - 3)).astype(F32).astype(BF16)
    squares = (dot(first, own, NT) + dot(second, other, NT)).astype(BF16)
    own, other = own[:, :FEAT], other[:, :FEAT]
    for place in range(CHIPS):
        columns = slice(place * HID_Y, (place + 1) * HID_Y)
        gate = dot(own, own_gate_ref[0, :, columns]) + dot(other, other_gate_ref[0, :, columns])
        up = dot(own, own_up_ref[0, :, columns]) + dot(other, other_up_ref[0, :, columns])
        out_ref[place, :CLASS, :] = gate.astype(BF16)
        out_ref[place, CLASS : 2 * CLASS, :] = up.astype(BF16)
        out_ref[place, 2 * CLASS :, :] = squares


def hidden_kernel(parts_ref, out_ref):
    gate = jnp.sum(parts_ref[:, :CLASS, :].astype(F32), axis=0)
    up = jnp.sum(parts_ref[:, CLASS : 2 * CLASS, :].astype(F32), axis=0)
    squares = jnp.sum(parts_ref[:, 2 * CLASS :, :].astype(F32), axis=0)
    squares = jnp.sum(squares[:6], axis=0, keepdims=True)
    diagonal = iota((CLASS, CLASS), 0) == iota((CLASS, CLASS), 1)
    squares = jnp.sum(jnp.where(diagonal, squares, 0.0), axis=1, keepdims=True)
    scale = lax.rsqrt(squares / D + EPS)
    gate = gate * scale
    hidden = (gate / (1.0 + jnp.exp(-gate)) * (up * scale)).astype(BF16)
    for place in range(CHIPS):
        out_ref[place] = hidden


def down_kernel(hidden_ref, own_ref, other_ref, out_ref):
    hidden = jnp.concatenate([hidden_ref[chip] for chip in range(CHIPS)], axis=1)
    shape = (4 * CLASS, 4 * CLASS)
    row, source = iota(shape, 0), iota(shape, 1)
    order = (source == row % 16 // 4 * CLASS + row // 16 * 4 + row % 4).astype(F32).astype(BF16)
    core = kv_index() % 2
    for weights_ref, whose in ((own_ref, core), (other_ref, 1 - core)):
        rows = dot(hidden, weights_ref[0], NT)
        rows = jnp.concatenate([rows, jnp.zeros((CLASS, 512 - FEAT), F32)], axis=1).astype(BF16)
        tiles = jnp.concatenate([rows[:, at * 128 : (at + 1) * 128] for at in range(4)], axis=0)
        place = pl.ds(pl.multiple_of(whose * N_TP, N_TP), N_TP)
        out_ref[place] = dot(order, tiles).reshape(N_TP, 16, 128).astype(BF16)


def mix_kernel(parts_ref, mine_ref, own_ref, other_ref, ids_ref, weights_ref, attended_ref, out_ref):
    own = own_ref[...].astype(F32)
    attended = jnp.where(own_half(own.shape, 0), own, swap_halves(other_ref[...].astype(F32)))
    attended_ref[...] = attended.astype(BF16)
    ids = ids_ref[...]
    weights = weights_ref[...]
    lane = iota((ROWS_TP, 128), 1)
    upper = iota((ROWS_TP, 128), 0) < ROWS_TP // 2
    shares = jnp.zeros(lane.shape, F32)
    for choice in range(ids.shape[1]):
        one = slice(choice, choice + 1)
        shares = jnp.where(ids[:, one] == lane, weights[:, one], shares)
    sums = []
    for core in range(2):
        mine = jnp.where(upper == (core == 0), shares, swap_halves(shares))
        mine = jnp.concatenate([mine, mine], axis=0)
        total = jnp.zeros((16, 128), F32)
        for expert in range(EXPERTS):
            at = core * N_TP + 2 * expert
            both = parts_ref[at].astype(F32) + parts_ref[at + 1].astype(F32)
            total = total + mine[:, expert : expert + 1] * both
        sums.append(total)
    tiles = []
    for at in range(2):
        first, second = (total[at * ROWS_TP : (at + 1) * ROWS_TP] for total in sums)
        tiles.append(jnp.where(upper, first, swap_halves(second)))
        tiles.append(jnp.where(upper, swap_halves(first), second))
    experts = jnp.concatenate(tiles, axis=1)[:, :FEAT]
    out_ref[...] = (from_tiles(mine_ref[TOKEN_AT:, :]) + attended + experts).astype(BF16)


def run(kernel, outs, *operands, fetched=(), left=0, scratch=(), cost=None, limit=24, after=()):
    single = not isinstance(outs, list)
    outs = [outs] if single else outs
    vmem, hbm, free = (pl.BlockSpec(memory_space=space) for space in (pltpu.VMEM, pltpu.HBM, pl.ANY))
    outs = outs[: len(outs) - left] + [pltpu.HBM(out.shape, out.dtype) for out in outs[len(outs) - left :]]
    placed = [vmem] * (len(outs) - left) + [hbm] * left
    count = len(operands) + len(fetched)

    def body(*refs):
        kernel(*refs[:count], *refs[count + len(after) :])

    return pl.pallas_call(
        body,
        out_shape=outs[0] if single else tuple(outs),
        in_specs=[vmem] * len(operands) + [free] * (len(fetched) + len(after)),
        out_specs=placed[0] if single else tuple(placed),
        scratch_shapes=list(scratch),
        cost_estimate=cost,
        compiler_params=pltpu.CompilerParams(vmem_limit_bytes=limit * 2**20),
    )(*operands, *fetched, *after)


def in_hbm(array):
    return pltpu.with_memory_space_constraint(array, pltpu.HBM)


def shaped(*shape, dtype=BF16):
    return jax.ShapeDtypeStruct(shape, dtype)


def start(tokens, attn_gain, down_kv, key_up, value_up, mlp_gain):
    return run(
        start_kernel, [shaped(CHIPS, UP_ROWS + FRESH_ROWS, 128), shaped(8 * ROWS_TP, 128, dtype=F32)],
        tokens, attn_gain.reshape(1, FEAT), down_kv, jnp.swapaxes(key_up, 1, 2), value_up,
        mlp_gain.reshape(1, FEAT), limit=60,
    )


def own_sum(ups, mine, after):
    return run(
        sum_kernel, shaped(PACK_ROWS, 128, dtype=F32), fetched=(ups, in_hbm(mine)), after=after,
        scratch=[
            pltpu.VMEM((CHIPS, FRESH_ROWS, 128), BF16), pltpu.VMEM(mine.shape, F32), pltpu.SemaphoreType.DMA((2,)),
        ],
    )


def fresh(own, other, latent_gain, lengths):
    freq = 10000.0 ** (-2.0 * jnp.arange(ROPE // 2, dtype=F32) / ROPE)
    return run(
        fresh_kernel, shaped(N_TP, ROWS_TP, KEY_W),
        own, other, latent_gain.reshape(1, LAT), lengths.reshape(1, SEQS), freq[None],
        left=1, scratch=[pltpu.VMEM((N_TP, ROWS_TP, KEY_W), BF16), pltpu.SemaphoreType.DMA],
    )


def attend(lengths, own, other, query_nope, query_rope, keys, other_keys):
    return run(
        attend_kernel,
        [
            shaped(CLASS, ATT_W),
            shaped(HEADS_DEV * ROWS_KV, KEY),
            shaped(HEADS_DEV, CHIPS, 2, LAT_KV, 128),
        ],
        lengths.reshape(1, SEQS),
        fetched=(own, other, in_hbm(query_nope), in_hbm(query_rope), in_hbm(keys), other_keys),
        left=2,
        scratch=[
            pltpu.VMEM((2 * HEADS_DEV, CHIPS, 2, LAT_KV, 128), BF16),
            pltpu.VMEM((HEADS_DEV * ROWS_KV, KEY), BF16),
            pltpu.VMEM((SEQS, HEADS_DEV * CLASS // SEQS, KEY), BF16),
            pltpu.VMEM(query_nope.shape, BF16),
            pltpu.VMEM(query_rope.shape, BF16),
            pltpu.VMEM(keys.shape, BF16),
            pltpu.VMEM(keys.shape, BF16),
            pltpu.SemaphoreType.DMA((6 + 4 * HEADS_DEV,)),
        ],
        cost=pl.CostEstimate(flops=2_200_000_000, bytes_accessed=4_000_000, transcendentals=800_000),
    )


def combine(parts, own, values, keys):
    return run(
        combine_kernel, shaped(CHIPS, ROWS_KV, HEADS_DEV * VDIM), parts, keys,
        fetched=(in_hbm(own), in_hbm(values)),
        scratch=[
            pltpu.VMEM(own.shape, BF16), pltpu.VMEM(values.shape, BF16), pltpu.SemaphoreType.DMA((2,)),
        ],
    )


def project(values, own, other):
    return run(project_kernel, shaped(N_TP, ROWS_TP, FEAT), values, own, other)


def route(parts, mine, other):
    return run(route_kernel, [shaped(ROWS_TP, FEAT), shaped(N_TP, ROWS_TP, 512)], parts, mine, other)


def gate(rows, own_gate, own_up, other_gate, other_up):
    return run(gate_kernel, shaped(CHIPS, PART_ROWS, 128), rows, own_gate, own_up, other_gate, other_up)


def hidden(parts):
    return run(hidden_kernel, shaped(CHIPS, CLASS, HID_Y), parts)


def down(packed, own, other):
    return run(down_kernel, shaped(2 * N_TP, 16, 128), packed, own, other)


def mix(parts, mine, own, other, expert_ids, expert_weights):
    outs = [shaped(ROWS_TP, FEAT), shaped(ROWS_TP, FEAT)]
    return run(mix_kernel, outs, parts, mine, own, other, expert_ids, expert_weights)


def exchange(array, axis, groups=None):
    return lax.all_to_all(array, axis, split_axis=0, concat_axis=0, axis_index_groups=groups, tiled=True)


def along_y(array):
    return exchange(array, "kv", [[2 * chip + core for chip in range(CHIPS)] for core in range(2)])


def to_owners(array):
    groups = [[(2 * chip + core) * N_TP + place for core in range(2) for place in range(N_TP)] for chip in range(CHIPS)]
    return exchange(array, ("kv", "tp"), groups)


def other_core(array):
    return lax.ppermute(array, "kv", [(index, index ^ 1) for index in range(N_KV)])


def per_device(
    tokens, attn_gain, down_kv, latent_gain, query_nope, query_rope, cache, lengths, key_up, value_up,
    out_proj, mlp_gain, expert_ids, expert_weights, gate_proj, up_proj, down_proj,
):
    ups, mine = start(tokens, attn_gain, down_kv, key_up, value_up, mlp_gain)
    own_cache, own_out, own_down = jnp.swapaxes(cache, 1, 2), out_proj.T, jnp.swapaxes(down_proj, 1, 2)
    ups, *moved = lax.optimization_barrier((ups, own_cache, own_out, gate_proj, up_proj, own_down))
    own = along_y(ups)
    moved = [other_core(array) for array in moved]
    other_cache, other_out, other_gate, other_up, other_down = moved
    mine = own_sum(own, mine, moved)
    other = other_core(mine)
    keys = fresh(mine, other, latent_gain, lengths)
    keys, own = lax.optimization_barrier((keys, own))
    keys = exchange(keys, "tp")
    parts, queries, values = attend(lengths, own, other_core(own), query_nope, query_rope, own_cache, other_cache)
    parts, keys = lax.optimization_barrier((parts, keys))
    parts = along_y(parts.reshape(CHIPS, ROWS_KV, ATT_W))
    values = along_y(combine(parts, queries, values, keys))
    parts = exchange(project(values, own_out, other_out), "tp")
    attended, rows = route(parts, mine, other)
    other_attended = other_core(attended)
    rows = exchange(rows, "tp")
    parts = along_y(gate(rows, gate_proj, up_proj, other_gate, other_up))
    packed = along_y(hidden(parts))
    parts = to_owners(down(packed, own_down, other_down))
    return mix(parts, mine, attended, other_attended, expert_ids, expert_weights)


def solution(mesh):
    return jax.shard_map(
        per_device,
        mesh=mesh,
        in_specs=(
            P("tp", "kv"),
            P("kv"),
            P("kv", None),
            P(),
            P(None, "tp"),
            P(None, "tp"),
            P(None, "kv", None),
            P(),
            P("tp", None, "kv"),
            P("tp", "kv", None),
            P("tp", "kv"),
            P("kv"),
            P("tp", None),
            P("tp", None),
            P("tp", "kv", None),
            P("tp", "kv", None),
            P("tp", None, "kv"),
        ),
        out_specs=(P("tp", "kv"), P("tp", "kv")),
        check_vma=False,
    )
```

```python
import functools
import math

import jax
import jax.numpy as jnp
from jax import lax
from jax.experimental import pallas as pl
from jax.experimental.pallas import tpu as pltpu
from jax.sharding import PartitionSpec as P

D = 7168
NOPE = 128
ROPE = 64
LAT = 512
VDIM = 128
SEQS = 2
QROWS = 32
STEPS = 4
TOKROWS = 256
EXPERTS = 16

N_KV = 16
N_TP = 32
HEADS_DEV = 4
FEAT = D // N_KV
ROWS_TP = TOKROWS // N_TP
ROWS_KV = TOKROWS // N_KV
KEY = LAT + ROPE
PAIRS = SEQS * QROWS
STAT = 2 * HEADS_DEV
ATT_W = LAT + 128
CHIPS = N_KV // 2
LAT_KV = LAT // N_KV
UP_ROWS = 2 * HEADS_DEV * LAT_KV
FRESH_W = KEY + ROPE
FRESH_ROWS = 48
TOKEN_AT = 0
GAIN_AT = TOKEN_AT + 4 * ROWS_TP
CLASS = TOKROWS // 2
PART_ROWS = 2 * CLASS + 16
KEY_W = 384
HID = 1024
HID_Y = HID // 8

EPS = 1e-06
LOWEST = -1e30
SCALE = 1.0 / math.sqrt(NOPE + ROPE)

F32 = jnp.float32
BF16 = jnp.bfloat16
NT = (((1,), (1,)), ((), ()))
TN = (((0,), (0,)), ((), ()))


def kv_index():
    return lax.axis_index("kv")


def tp_index():
    return lax.axis_index("tp")


def iota(shape, dim):
    return lax.broadcasted_iota(jnp.int32, shape, dim)


def dot(a, b, dims=(((1,), (0,)), ((), ()))):
    return lax.dot_general(a, b, dims, preferred_element_type=F32)


def parts_of(value):
    high = value.astype(BF16).astype(F32)
    rest = value - high
    middle = rest.astype(BF16).astype(F32)
    return high, middle, rest - middle


def with_stats(stats, head, peak, total):
    lane = iota(stats.shape, 1)
    for at, part in enumerate(parts_of(peak)):
        stats = jnp.where(lane == at * STAT + head, part, stats)
    for at, part in enumerate(parts_of(total)):
        stats = jnp.where(lane == at * STAT + HEADS_DEV + head, part, stats)
    return stats


def whole_stats(tail):
    return tail[..., :STAT] + tail[..., STAT : 2 * STAT] + tail[..., 2 * STAT : 3 * STAT]


def swap_halves(rows):
    return pltpu.roll(rows, 4, 0)


def in_tiles(rows):
    rows = jnp.concatenate([rows, jnp.zeros((ROWS_TP, 512 - FEAT), F32)], axis=1)
    return [rows[:, at * 128 : (at + 1) * 128] for at in range(4)]


def from_tiles(tiles):
    return jnp.concatenate([tiles[at * ROWS_TP : (at + 1) * ROWS_TP] for at in range(4)], axis=1)[:, :FEAT]


def start_kernel(tokens_ref, gain_ref, down_ref, key_ref, value_ref, mlp_gain_ref, out_ref, mine_ref):
    wide_tokens = tokens_ref[...].astype(F32)
    mine_ref[...] = jnp.concatenate(
        in_tiles(wide_tokens) + in_tiles(jnp.broadcast_to(mlp_gain_ref[...], (ROWS_TP, FEAT))), axis=0
    )
    normed = (wide_tokens * gain_ref[...]).astype(BF16)
    fresh = dot(normed, down_ref[...])
    fresh = jnp.concatenate([fresh, jnp.zeros((ROWS_TP, ROPE), F32)], axis=1)
    tiles = [fresh[:, at * 128 : (at + 1) * 128] for at in range(FRESH_W // 128)]
    tiles.append(jnp.zeros((FRESH_ROWS - ROWS_TP * len(tiles), 128), F32))
    packed = jnp.concatenate(tiles, axis=0).astype(BF16)
    for place in range(CHIPS):
        for head in range(HEADS_DEV):
            out_ref[place, head * LAT_KV : (head + 1) * LAT_KV, :] = key_ref[head]
            out_ref[place, UP_ROWS // 2 + head * LAT_KV : UP_ROWS // 2 + (head + 1) * LAT_KV, :] = value_ref[head]
        out_ref[place, UP_ROWS:, :] = packed


def fresh_kernel(gain_ref, lengths_ref, freq_ref, own_hbm, other_hbm, out_hbm, own_ref, other_ref, out_ref, sems):
    rows = pl.ds(UP_ROWS, FRESH_ROWS)
    fetches = [
        pltpu.make_async_copy(own_hbm.at[:, rows, :], own_ref, sems.at[0]),
        pltpu.make_async_copy(other_hbm.at[:, rows, :], other_ref, sems.at[1]),
    ]
    for fetch in fetches:
        fetch.start()
    for fetch in fetches:
        fetch.wait()
    packed = jnp.sum(own_ref[...].astype(F32), axis=0) + jnp.sum(other_ref[...].astype(F32), axis=0)
    tiles = [packed[at * ROWS_TP : (at + 1) * ROWS_TP] for at in range(FRESH_W // 128)]
    fresh = jnp.concatenate(tiles[:-1], axis=1)
    turn = tiles[-1][:, :ROPE]
    scaled = fresh * lax.rsqrt(jnp.mean(fresh * fresh, axis=1, keepdims=True) + EPS) * gain_ref[...]
    row = tp_index() * ROWS_TP
    lengths = lengths_ref[...]
    start = jnp.where(row // QROWS % SEQS == 0, lengths[:, 0:1], lengths[:, 1:2])
    angle = (start + row // PAIRS).astype(F32) * freq_ref[...]
    cosine, sine = jnp.cos(angle), jnp.sin(angle)
    first, second = turn[:, : ROPE // 2], turn[:, ROPE // 2 :]
    turned = [first * cosine - second * sine, second * cosine + first * sine]
    key = jnp.concatenate([scaled] + turned + [jnp.zeros((ROWS_TP, ROPE), F32)], axis=1)
    key = jnp.where(kv_index() % 2 == 0, key, swap_halves(key))
    upper = jnp.concatenate([key[:, :256], key[:, LAT:]], axis=1)
    lower = jnp.concatenate([swap_halves(key[:, 256:LAT]), jnp.zeros((ROWS_TP, KEY_W - 256), F32)], axis=1)
    key = jnp.where(iota(upper.shape, 0) < ROWS_TP // 2, upper, lower).astype(BF16)
    for place in range(N_TP):
        out_ref[place] = key
    leave = pltpu.make_async_copy(out_ref, out_hbm, sems.at[2])
    leave.start()
    leave.wait()


def attend_kernel(
    lengths_ref, own_ups_hbm, other_ups_hbm, nope_hbm, rope_hbm, keys_hbm, other_keys_hbm,
    out_ref, own_hbm, values_hbm, ups_ref, own_ref, queries, nope_ref, rope_ref, keys_ref, other_keys_ref, sems,
):
    kv = kv_index()
    core = kv % 2
    waits = []

    def fetch(source, target):
        waits.append(pltpu.make_async_copy(source, target, sems.at[len(waits)]))
        waits[-1].start()

    fetch(nope_hbm, nope_ref)
    fetch(rope_hbm, rope_ref)
    for which in range(2 * HEADS_DEV):
        rows = pl.ds(which * LAT_KV, LAT_KV)
        fetch(own_ups_hbm.at[:, rows, :], ups_ref.at[which, :, core])
        fetch(other_ups_hbm.at[:, rows, :], ups_ref.at[which, :, 1 - core])
    fetch(keys_hbm, keys_ref)
    fetch(other_keys_hbm, other_keys_ref)
    row, source = iota((CLASS, TOKROWS), 0), iota((CLASS, TOKROWS), 1)
    pair = row // ROWS_KV * ROWS_TP + core * (ROWS_TP // 2) + row % ROWS_KV // STEPS
    reorder = (source == row % STEPS * PAIRS + pair).astype(F32).astype(BF16)
    rows_seq = CLASS // SEQS
    for wait in waits[:-2]:
        wait.wait()
    nope = dot(reorder, nope_ref[...]).astype(BF16)
    rope = dot(reorder, rope_ref[...]).astype(BF16)
    for head in range(HEADS_DEV):
        key_up = ups_ref[head].reshape(LAT, NOPE)
        absorbed = dot(nope[:, head * NOPE : (head + 1) * NOPE], key_up, NT).astype(BF16)
        turned = rope[:, head * ROPE : (head + 1) * ROPE]
        for seq in range(SEQS):
            rows = slice(seq * rows_seq, (seq + 1) * rows_seq)
            place = slice(head * rows_seq, (head + 1) * rows_seq)
            queries[seq, place, :LAT] = absorbed[rows]
            queries[seq, place, LAT:] = turned[rows]
    own_seq = kv // (N_KV // SEQS)
    own_row = kv // 2 % (CHIPS // SEQS) * ROWS_KV
    for head in range(HEADS_DEV):
        begin = pl.multiple_of(head * rows_seq + own_row, ROWS_KV)
        own_ref[head * ROWS_KV : (head + 1) * ROWS_KV, :] = queries[own_seq, pl.ds(begin, ROWS_KV), :]
    leaves = [
        pltpu.make_async_copy(own_ref, own_hbm, sems.at[len(waits)]),
        pltpu.make_async_copy(ups_ref.at[pl.ds(HEADS_DEV, HEADS_DEV)], values_hbm, sems.at[len(waits) + 1]),
    ]
    for leave in leaves:
        leave.start()
    for wait in waits[-2:]:
        wait.wait()
    span = keys_ref.shape[2]
    lengths = lengths_ref[...]
    for seq in range(SEQS):
        blocks = []
        for keys, index in ((keys_ref, kv), (other_keys_ref, kv + 1 - 2 * core)):
            valid = index * span + iota((1, span), 1) < lengths[:, seq : seq + 1]
            scores = dot(queries[seq], keys[seq]) * SCALE + jnp.where(valid, 0.0, LOWEST)
            blocks.append((keys, valid, scores, jnp.max(scores, axis=1, keepdims=True)))
        peak = jnp.maximum(blocks[0][3], blocks[1][3])
        total, latent = 0.0, 0.0
        for keys, valid, scores, _ in blocks:
            weights = jnp.where(valid, jnp.exp(scores - peak), 0.0).astype(BF16)
            total = total + jnp.sum(weights.astype(F32), axis=1, keepdims=True)
            latent = latent + dot(weights, keys[seq, :LAT, :], NT)
        latent = latent.astype(BF16)
        stats = jnp.zeros((rows_seq, 128), F32)
        rows = slice(seq * rows_seq, (seq + 1) * rows_seq)
        for head in range(HEADS_DEV):
            place = slice(head * rows_seq, (head + 1) * rows_seq)
            value_up = ups_ref[HEADS_DEV + head].reshape(LAT, VDIM)
            out_ref[rows, head * VDIM : (head + 1) * VDIM] = dot(latent[place], value_up).astype(BF16)
            stats = with_stats(stats, head, peak[place], total[place])
        out_ref[rows, LAT:] = stats.astype(BF16)
    for leave in leaves:
        leave.wait()


def combine_kernel(parts_ref, keys_ref, own_hbm, values_hbm, out_ref, own_ref, values_ref, sems):
    fetches = [
        pltpu.make_async_copy(own_hbm, own_ref, sems.at[0]),
        pltpu.make_async_copy(values_hbm, values_ref, sems.at[1]),
    ]
    for fetch in fetches:
        fetch.start()
    kv = kv_index()
    stats = whole_stats(parts_ref[:, :, LAT:].astype(F32))
    keys = []
    for step in range(STEPS):
        block = keys_ref[step * (PAIRS // ROWS_TP) + kv // 2].astype(F32)
        keys.append(jnp.concatenate([block[:, :256], swap_halves(block[:, :256]), block[:, 256 : 256 + ROPE]], axis=1))
    keys = jnp.concatenate(keys, axis=0).astype(BF16)
    for fetch in fetches:
        fetch.wait()
    scores = dot(own_ref[...], keys, NT) * SCALE
    row = iota(scores.shape, 0) % ROWS_KV
    key = iota(scores.shape, 1)
    causal = (row // STEPS == key % ROWS_TP) & (key // ROWS_TP <= row % STEPS)
    scores = jnp.where(causal, scores, LOWEST)
    fresh_peak = jnp.max(scores, axis=1, keepdims=True)
    weights = jnp.where(causal, jnp.exp(scores - fresh_peak), 0.0).astype(BF16)
    fresh_total = jnp.sum(weights.astype(F32), axis=1, keepdims=True)
    fresh_latent = dot(weights, keys[:, :LAT]).astype(BF16)
    for head in range(HEADS_DEV):
        own = slice(head * ROWS_KV, (head + 1) * ROWS_KV)
        peak = stats[:, :, head : head + 1]
        total = stats[:, :, HEADS_DEV + head : HEADS_DEV + head + 1]
        top = jnp.maximum(jnp.max(peak, axis=0), fresh_peak[own])
        keep = jnp.exp(peak - top[None])
        fresh_keep = jnp.exp(fresh_peak[own] - top)
        value_up = values_ref[head].reshape(LAT, VDIM)
        part = parts_ref[:, :, head * VDIM : (head + 1) * VDIM].astype(F32)
        value = jnp.sum(part * keep, axis=0) + dot(fresh_latent[own], value_up) * fresh_keep
        whole = jnp.sum(total * keep, axis=0) + fresh_total[own] * fresh_keep
        value = (value / whole).astype(BF16)
        for place in range(CHIPS):
            out_ref[place, :, head * VDIM : (head + 1) * VDIM] = value


def own_half(shape, dim):
    return iota(shape, dim) % ROWS_TP // (ROWS_TP // 2) == kv_index() % 2


def project_kernel(values_ref, own_ref, other_ref, out_ref):
    values = values_ref[...].reshape(CLASS, HEADS_DEV * VDIM)
    shape = (TOKROWS, CLASS)
    row, source = iota(shape, 0), iota(shape, 1)
    block, pair = row // ROWS_TP, row % (ROWS_TP // 2)
    match = source == block % CHIPS * ROWS_KV + pair * STEPS + block // CHIPS
    own = (match & own_half(shape, 0)).astype(F32).astype(BF16)
    other = (match & ~own_half(shape, 0)).astype(F32).astype(BF16)
    out = dot(dot(own, values).astype(BF16), own_ref[...], NT)
    out = out + dot(dot(other, values).astype(BF16), other_ref[...], NT)
    out_ref[...] = out.reshape(N_TP, ROWS_TP, FEAT).astype(BF16)


def route_kernel(parts_ref, mine_ref, other_ref, attended_ref, out_ref):
    attended = jnp.sum(parts_ref[...].astype(F32), axis=0).astype(BF16)
    attended_ref[...] = attended
    own = own_half((ROWS_TP, FEAT), 0)
    tokens = jnp.where(own, from_tiles(mine_ref[TOKEN_AT:, :]), swap_halves(from_tiles(other_ref[TOKEN_AT:, :])))
    gain = jnp.where(own, from_tiles(mine_ref[GAIN_AT:, :]), from_tiles(other_ref[GAIN_AT:, :]))
    mid = tokens + attended.astype(F32)
    lane = iota((ROWS_TP, 512 - FEAT), 1)
    extra = jnp.zeros(lane.shape, F32)
    for at, part in enumerate(parts_of(jnp.sum(mid * mid, axis=1, keepdims=True))):
        extra = jnp.where(lane == at, part, extra)
    row_data = jnp.concatenate([mid * gain, extra], axis=1).astype(BF16)
    for place in range(N_TP):
        out_ref[place] = row_data


def gate_kernel(
    rows_ref, other_gate_ref, other_up_ref, own_gate_hbm, own_up_hbm, out_ref, own_gate_ref, own_up_ref, sems,
):
    fetches = []
    for place in range(CHIPS):
        columns = pl.ds(place * HID_Y, HID_Y)
        for source, target in ((own_gate_hbm, own_gate_ref), (own_up_hbm, own_up_ref)):
            at = (0, slice(None), columns)
            fetches.append(pltpu.make_async_copy(source.at[at], target.at[at], sems.at[len(fetches)]))
            fetches[-1].start()
    rows = rows_ref[...].astype(F32).reshape(TOKROWS, 512).astype(BF16)
    shape = (CLASS, TOKROWS)
    place, row = iota(shape, 0), iota(shape, 1)
    match = place == row // ROWS_TP * (ROWS_TP // 2) + row % (ROWS_TP // 2)
    own = dot((match & own_half(shape, 1)).astype(F32).astype(BF16), rows).astype(BF16)
    other = dot((match & ~own_half(shape, 1)).astype(F32).astype(BF16), rows).astype(BF16)
    sixteen, column = iota((16, 512), 0), iota((16, 512), 1)
    first = ((sixteen < 3) & (column == FEAT + sixteen)).astype(F32).astype(BF16)
    second = ((sixteen >= 3) & (sixteen < 6) & (column == FEAT + sixteen - 3)).astype(F32).astype(BF16)
    squares = (dot(first, own, NT) + dot(second, other, NT)).astype(BF16)
    own, other = own[:, :FEAT], other[:, :FEAT]
    for place in range(CHIPS):
        columns = slice(place * HID_Y, (place + 1) * HID_Y)
        fetches[2 * place].wait()
        fetches[2 * place + 1].wait()
        gate = dot(own, own_gate_ref[0, :, columns]) + dot(other, other_gate_ref[0, :, columns])
        up = dot(own, own_up_ref[0, :, columns]) + dot(other, other_up_ref[0, :, columns])
        out_ref[place, :CLASS, :] = gate.astype(BF16)
        out_ref[place, CLASS : 2 * CLASS, :] = up.astype(BF16)
        out_ref[place, 2 * CLASS :, :] = squares


def hidden_kernel(parts_ref, out_ref):
    gate = jnp.sum(parts_ref[:, :CLASS, :].astype(F32), axis=0)
    up = jnp.sum(parts_ref[:, CLASS : 2 * CLASS, :].astype(F32), axis=0)
    squares = jnp.sum(parts_ref[:, 2 * CLASS :, :].astype(F32), axis=0)
    squares = jnp.sum(squares[:6], axis=0, keepdims=True)
    diagonal = iota((CLASS, CLASS), 0) == iota((CLASS, CLASS), 1)
    squares = jnp.sum(jnp.where(diagonal, squares, 0.0), axis=1, keepdims=True)
    scale = lax.rsqrt(squares / D + EPS)
    gate = gate * scale
    hidden = (gate / (1.0 + jnp.exp(-gate)) * (up * scale)).astype(BF16)
    for place in range(CHIPS):
        out_ref[place] = hidden


def down_kernel(hidden_ref, weights_ref, out_ref):
    hidden = jnp.concatenate([hidden_ref[chip] for chip in range(CHIPS)], axis=1)
    out_ref[...] = dot(hidden, weights_ref[0], NT).astype(BF16)


def join_kernel(own_ref, came_ref, out_ref):
    shape = (TOKROWS, CLASS)
    row, source = iota(shape, 0), iota(shape, 1)
    match = source == row // ROWS_TP * (ROWS_TP // 2) + row % (ROWS_TP // 2)
    own = (match & own_half(shape, 0)).astype(F32).astype(BF16)
    other = (match & ~own_half(shape, 0)).astype(F32).astype(BF16)
    out = dot(own, own_ref[...]) + dot(other, came_ref[...])
    out_ref[...] = out.reshape(N_TP, ROWS_TP, FEAT).astype(BF16)


def mix_kernel(parts_ref, mine_ref, own_ref, other_ref, ids_ref, weights_ref, attended_ref, out_ref):
    own = own_ref[...].astype(F32)
    attended = jnp.where(own_half(own.shape, 0), own, swap_halves(other_ref[...].astype(F32)))
    attended_ref[...] = attended.astype(BF16)
    total = from_tiles(mine_ref[TOKEN_AT:, :]) + attended
    ids = ids_ref[...]
    weights = weights_ref[...]
    for expert in range(EXPERTS):
        share = jnp.sum(jnp.where(ids == expert, weights, 0.0), axis=1, keepdims=True)
        both = parts_ref[2 * expert].astype(F32) + parts_ref[2 * expert + 1].astype(F32)
        total = total + share * both
    out_ref[...] = total.astype(BF16)


def run(kernel, outs, *operands, fetched=(), left=0, scratch=(), cost=None, limit=24, after=()):
    single = not isinstance(outs, list)
    outs = [outs] if single else outs
    vmem, hbm, free = (pl.BlockSpec(memory_space=space) for space in (pltpu.VMEM, pltpu.HBM, pl.ANY))
    outs = outs[: len(outs) - left] + [pltpu.HBM(out.shape, out.dtype) for out in outs[len(outs) - left :]]
    placed = [vmem] * (len(outs) - left) + [hbm] * left
    count = len(operands) + len(fetched)

    def body(*refs):
        kernel(*refs[:count], *refs[count + len(after) :])

    return pl.pallas_call(
        body,
        out_shape=outs[0] if single else tuple(outs),
        in_specs=[vmem] * len(operands) + [free] * (len(fetched) + len(after)),
        out_specs=placed[0] if single else tuple(placed),
        scratch_shapes=list(scratch),
        cost_estimate=cost,
        compiler_params=pltpu.CompilerParams(vmem_limit_bytes=limit * 2**20),
    )(*operands, *fetched, *after)


def in_hbm(array):
    return pltpu.with_memory_space_constraint(array, pltpu.HBM)


def shaped(*shape, dtype=BF16):
    return jax.ShapeDtypeStruct(shape, dtype)


def start(tokens, attn_gain, down_kv, key_up, value_up, mlp_gain):
    return run(
        start_kernel, [shaped(CHIPS, UP_ROWS + FRESH_ROWS, 128), shaped(8 * ROWS_TP, 128, dtype=F32)],
        tokens, attn_gain.reshape(1, FEAT), down_kv, jnp.swapaxes(key_up, 1, 2), value_up,
        mlp_gain.reshape(1, FEAT), limit=60,
    )


def fresh(own, other, latent_gain, lengths):
    freq = 10000.0 ** (-2.0 * jnp.arange(ROPE // 2, dtype=F32) / ROPE)
    part = pltpu.VMEM((CHIPS, FRESH_ROWS, 128), BF16)
    return run(
        fresh_kernel, shaped(N_TP, ROWS_TP, KEY_W),
        latent_gain.reshape(1, LAT), lengths.reshape(1, SEQS), freq[None], fetched=(own, other),
        left=1, scratch=[part, part, pltpu.VMEM((N_TP, ROWS_TP, KEY_W), BF16), pltpu.SemaphoreType.DMA((3,))],
    )


def attend(lengths, own, other, query_nope, query_rope, keys, other_keys):
    return run(
        attend_kernel,
        [
            shaped(CLASS, ATT_W),
            shaped(HEADS_DEV * ROWS_KV, KEY),
            shaped(HEADS_DEV, CHIPS, 2, LAT_KV, 128),
        ],
        lengths.reshape(1, SEQS),
        fetched=(own, other, in_hbm(query_nope), in_hbm(query_rope), in_hbm(keys), other_keys),
        left=2,
        scratch=[
            pltpu.VMEM((2 * HEADS_DEV, CHIPS, 2, LAT_KV, 128), BF16),
            pltpu.VMEM((HEADS_DEV * ROWS_KV, KEY), BF16),
            pltpu.VMEM((SEQS, HEADS_DEV * CLASS // SEQS, KEY), BF16),
            pltpu.VMEM(query_nope.shape, BF16),
            pltpu.VMEM(query_rope.shape, BF16),
            pltpu.VMEM(keys.shape, BF16),
            pltpu.VMEM(keys.shape, BF16),
            pltpu.SemaphoreType.DMA((6 + 4 * HEADS_DEV,)),
        ],
        cost=pl.CostEstimate(flops=2_200_000_000, bytes_accessed=4_000_000, transcendentals=800_000),
    )


def combine(parts, own, values, keys):
    return run(
        combine_kernel, shaped(CHIPS, ROWS_KV, HEADS_DEV * VDIM), parts, keys,
        fetched=(in_hbm(own), in_hbm(values)),
        scratch=[
            pltpu.VMEM(own.shape, BF16), pltpu.VMEM(values.shape, BF16), pltpu.SemaphoreType.DMA((2,)),
        ],
    )


def project(values, own, other):
    return run(project_kernel, shaped(N_TP, ROWS_TP, FEAT), values, own, other)


def route(parts, mine, other):
    return run(route_kernel, [shaped(ROWS_TP, FEAT), shaped(N_TP, ROWS_TP, 512)], parts, mine, other)


def gate(rows, own_gate, own_up, other_gate, other_up):
    weights = pltpu.VMEM(own_gate.shape, BF16)
    return run(
        gate_kernel, shaped(CHIPS, PART_ROWS, 128), rows, other_gate, other_up,
        fetched=(in_hbm(own_gate), in_hbm(own_up)), scratch=[weights, weights, pltpu.SemaphoreType.DMA((2 * CHIPS,))],
    )


def hidden(parts):
    return run(hidden_kernel, shaped(CHIPS, CLASS, HID_Y), parts)


def down(packed, weights):
    return run(down_kernel, shaped(CLASS, FEAT), packed, weights)


def join(own, came):
    return run(join_kernel, shaped(N_TP, ROWS_TP, FEAT), own, came)


def mix(parts, mine, own, other, expert_ids, expert_weights):
    outs = [shaped(ROWS_TP, FEAT), shaped(ROWS_TP, FEAT)]
    return run(mix_kernel, outs, parts, mine, own, other, expert_ids, expert_weights)


def exchange(array, axis, groups=None):
    return lax.all_to_all(array, axis, split_axis=0, concat_axis=0, axis_index_groups=groups, tiled=True)


def along_y(array):
    return exchange(array, "kv", [[2 * chip + core for chip in range(CHIPS)] for core in range(2)])


def other_core(array):
    return lax.ppermute(array, "kv", [(index, index ^ 1) for index in range(N_KV)])


def per_device(
    tokens, attn_gain, down_kv, latent_gain, query_nope, query_rope, cache, lengths, key_up, value_up,
    out_proj, mlp_gain, expert_ids, expert_weights, gate_proj, up_proj, down_proj,
):
    ups, mine = start(tokens, attn_gain, down_kv, key_up, value_up, mlp_gain)
    own_cache, own_out, own_down = jnp.swapaxes(cache, 1, 2), out_proj.T, jnp.swapaxes(down_proj, 1, 2)
    ups, waiting, *moved = lax.optimization_barrier((ups, own_cache, own_out, mine, gate_proj, up_proj, own_down))
    own = along_y(ups)
    moved = [other_core(array) for array in moved]
    other_out, other_mine, other_gate, other_up, other_down = moved
    other_cache = other_core(waiting)
    own, *moved = lax.optimization_barrier((own, other_out, other_mine, other_gate, other_up, other_down))
    other_out, other_mine, other_gate, other_up, other_down = moved
    other = other_core(own)
    keys = fresh(own, other, latent_gain, lengths)
    keys, own, other = lax.optimization_barrier((keys, own, other))
    keys = exchange(keys, "tp")
    parts, queries, values = attend(lengths, own, other, query_nope, query_rope, own_cache, other_cache)
    parts, keys = lax.optimization_barrier((parts, keys))
    parts = along_y(parts.reshape(CHIPS, ROWS_KV, ATT_W))
    values = along_y(combine(parts, queries, values, keys))
    parts = exchange(project(values, own_out, other_out), "tp")
    attended, rows = route(parts, mine, other_mine)
    rows = exchange(rows, "tp")
    parts = along_y(gate(rows, gate_proj, up_proj, other_gate, other_up))
    packed = along_y(hidden(parts))
    came = other_core(down(packed, other_down))
    parts, leaving = lax.optimization_barrier((join(down(packed, own_down), came), attended))
    other_attended = other_core(leaving)
    parts = exchange(parts, "tp")
    return mix(parts, mine, attended, other_attended, expert_ids, expert_weights)


def solution(mesh):
    return jax.shard_map(
        per_device,
        mesh=mesh,
        in_specs=(
            P("tp", "kv"),
            P("kv"),
            P("kv", None),
            P(),
            P(None, "tp"),
            P(None, "tp"),
            P(None, "kv", None),
            P(),
            P("tp", None, "kv"),
            P("tp", "kv", None),
            P("tp", "kv"),
            P("kv"),
            P("tp", None),
            P("tp", None),
            P("tp", "kv", None),
            P("tp", "kv", None),
            P("tp", None, "kv"),
        ),
        out_specs=(P("tp", "kv"), P("tp", "kv")),
        check_vma=False,
    )
```

```python
import functools
import math

import jax
import jax.numpy as jnp
from jax import lax
from jax.experimental import pallas as pl
from jax.experimental.pallas import tpu as pltpu
from jax.sharding import PartitionSpec as P

D = 7168
NOPE = 128
ROPE = 64
LAT = 512
VDIM = 128
SEQS = 2
QROWS = 32
STEPS = 4
TOKROWS = 256
EXPERTS = 16

N_KV = 16
N_TP = 32
HEADS_DEV = 4
FEAT = D // N_KV
ROWS_TP = TOKROWS // N_TP
ROWS_KV = TOKROWS // N_KV
KEY = LAT + ROPE
PAIRS = SEQS * QROWS
STAT = 2 * HEADS_DEV
ATT_W = LAT + 128
CHIPS = N_KV // 2
LAT_KV = LAT // N_KV
UP_ROWS = 2 * HEADS_DEV * LAT_KV
FRESH_W = KEY + ROPE
FRESH_ROWS = 48
TOKEN_AT = 0
GAIN_AT = TOKEN_AT + 4 * ROWS_TP
CLASS = TOKROWS // 2
PART_ROWS = 2 * CLASS + 16
KEY_W = 384
HID = 1024
HID_Y = HID // 8

EPS = 1e-06
LOWEST = -1e30
SCALE = 1.0 / math.sqrt(NOPE + ROPE)

F32 = jnp.float32
BF16 = jnp.bfloat16
NT = (((1,), (1,)), ((), ()))
TN = (((0,), (0,)), ((), ()))


def kv_index():
    return lax.axis_index("kv")


def tp_index():
    return lax.axis_index("tp")


def iota(shape, dim):
    return lax.broadcasted_iota(jnp.int32, shape, dim)


def dot(a, b, dims=(((1,), (0,)), ((), ()))):
    return lax.dot_general(a, b, dims, preferred_element_type=F32)


def parts_of(value):
    high = value.astype(BF16).astype(F32)
    rest = value - high
    middle = rest.astype(BF16).astype(F32)
    return high, middle, rest - middle


def with_stats(stats, head, peak, total):
    lane = iota(stats.shape, 1)
    for at, part in enumerate(parts_of(peak)):
        stats = jnp.where(lane == at * STAT + head, part, stats)
    for at, part in enumerate(parts_of(total)):
        stats = jnp.where(lane == at * STAT + HEADS_DEV + head, part, stats)
    return stats


def whole_stats(tail):
    return tail[..., :STAT] + tail[..., STAT : 2 * STAT] + tail[..., 2 * STAT : 3 * STAT]


def swap_halves(rows):
    return pltpu.roll(rows, 4, 0)


def in_tiles(rows):
    rows = jnp.concatenate([rows, jnp.zeros((ROWS_TP, 512 - FEAT), F32)], axis=1)
    return [rows[:, at * 128 : (at + 1) * 128] for at in range(4)]


def from_tiles(tiles):
    return jnp.concatenate([tiles[at * ROWS_TP : (at + 1) * ROWS_TP] for at in range(4)], axis=1)[:, :FEAT]


def start_kernel(tokens_ref, gain_ref, down_ref, key_ref, value_ref, mlp_gain_ref, out_ref, mine_ref):
    wide_tokens = tokens_ref[...].astype(F32)
    mine_ref[...] = jnp.concatenate(
        in_tiles(wide_tokens) + in_tiles(jnp.broadcast_to(mlp_gain_ref[...], (ROWS_TP, FEAT))), axis=0
    )
    normed = (wide_tokens * gain_ref[...]).astype(BF16)
    fresh = dot(normed, down_ref[...])
    fresh = jnp.concatenate([fresh, jnp.zeros((ROWS_TP, ROPE), F32)], axis=1)
    tiles = [fresh[:, at * 128 : (at + 1) * 128] for at in range(FRESH_W // 128)]
    tiles.append(jnp.zeros((FRESH_ROWS - ROWS_TP * len(tiles), 128), F32))
    packed = jnp.concatenate(tiles, axis=0).astype(BF16)
    for place in range(CHIPS):
        for head in range(HEADS_DEV):
            out_ref[place, head * LAT_KV : (head + 1) * LAT_KV, :] = key_ref[head]
            out_ref[place, UP_ROWS // 2 + head * LAT_KV : UP_ROWS // 2 + (head + 1) * LAT_KV, :] = value_ref[head]
        out_ref[place, UP_ROWS:, :] = packed


def fresh_kernel(gain_ref, lengths_ref, freq_ref, own_hbm, other_hbm, out_hbm, own_ref, other_ref, out_ref, sems):
    rows = pl.ds(UP_ROWS, FRESH_ROWS)
    fetches = [
        pltpu.make_async_copy(own_hbm.at[:, rows, :], own_ref, sems.at[0]),
        pltpu.make_async_copy(other_hbm.at[:, rows, :], other_ref, sems.at[1]),
    ]
    for fetch in fetches:
        fetch.start()
    for fetch in fetches:
        fetch.wait()
    packed = jnp.sum(own_ref[...].astype(F32), axis=0) + jnp.sum(other_ref[...].astype(F32), axis=0)
    tiles = [packed[at * ROWS_TP : (at + 1) * ROWS_TP] for at in range(FRESH_W // 128)]
    fresh = jnp.concatenate(tiles[:-1], axis=1)
    turn = tiles[-1][:, :ROPE]
    scaled = fresh * lax.rsqrt(jnp.mean(fresh * fresh, axis=1, keepdims=True) + EPS) * gain_ref[...]
    row = tp_index() * ROWS_TP
    lengths = lengths_ref[...]
    start = jnp.where(row // QROWS % SEQS == 0, lengths[:, 0:1], lengths[:, 1:2])
    angle = (start + row // PAIRS).astype(F32) * freq_ref[...]
    cosine, sine = jnp.cos(angle), jnp.sin(angle)
    first, second = turn[:, : ROPE // 2], turn[:, ROPE // 2 :]
    turned = [first * cosine - second * sine, second * cosine + first * sine]
    key = jnp.concatenate([scaled] + turned + [jnp.zeros((ROWS_TP, ROPE), F32)], axis=1)
    key = jnp.where(kv_index() % 2 == 0, key, swap_halves(key))
    upper = jnp.concatenate([key[:, :256], key[:, LAT:]], axis=1)
    lower = jnp.concatenate([swap_halves(key[:, 256:LAT]), jnp.zeros((ROWS_TP, KEY_W - 256), F32)], axis=1)
    key = jnp.where(iota(upper.shape, 0) < ROWS_TP // 2, upper, lower).astype(BF16)
    for place in range(N_TP):
        out_ref[place] = key
    leave = pltpu.make_async_copy(out_ref, out_hbm, sems.at[2])
    leave.start()
    leave.wait()


def attend_kernel(
    lengths_ref, own_ups_hbm, other_ups_hbm, nope_hbm, rope_hbm, keys_hbm, other_keys_hbm,
    out_ref, own_hbm, values_hbm, ups_ref, own_ref, queries, nope_ref, rope_ref, keys_ref, other_keys_ref, sems,
):
    kv = kv_index()
    core = kv % 2
    waits = []

    def fetch(source, target):
        waits.append(pltpu.make_async_copy(source, target, sems.at[len(waits)]))
        waits[-1].start()

    fetch(nope_hbm, nope_ref)
    fetch(rope_hbm, rope_ref)
    for which in range(2 * HEADS_DEV):
        rows = pl.ds(which * LAT_KV, LAT_KV)
        fetch(own_ups_hbm.at[:, rows, :], ups_ref.at[which, :, core])
        fetch(other_ups_hbm.at[:, rows, :], ups_ref.at[which, :, 1 - core])
    fetch(keys_hbm, keys_ref)
    fetch(other_keys_hbm, other_keys_ref)
    row, source = iota((CLASS, TOKROWS), 0), iota((CLASS, TOKROWS), 1)
    pair = row // ROWS_KV * ROWS_TP + core * (ROWS_TP // 2) + row % ROWS_KV // STEPS
    reorder = (source == row % STEPS * PAIRS + pair).astype(F32).astype(BF16)
    rows_seq = CLASS // SEQS
    for wait in waits[:-2]:
        wait.wait()
    nope = dot(reorder, nope_ref[...]).astype(BF16)
    rope = dot(reorder, rope_ref[...]).astype(BF16)
    for head in range(HEADS_DEV):
        key_up = ups_ref[head].reshape(LAT, NOPE)
        absorbed = dot(nope[:, head * NOPE : (head + 1) * NOPE], key_up, NT).astype(BF16)
        turned = rope[:, head * ROPE : (head + 1) * ROPE]
        for seq in range(SEQS):
            rows = slice(seq * rows_seq, (seq + 1) * rows_seq)
            place = slice(head * rows_seq, (head + 1) * rows_seq)
            queries[seq, place, :LAT] = absorbed[rows]
            queries[seq, place, LAT:] = turned[rows]
    own_seq = kv // (N_KV // SEQS)
    own_row = kv // 2 % (CHIPS // SEQS) * ROWS_KV
    for head in range(HEADS_DEV):
        begin = pl.multiple_of(head * rows_seq + own_row, ROWS_KV)
        own_ref[head * ROWS_KV : (head + 1) * ROWS_KV, :] = queries[own_seq, pl.ds(begin, ROWS_KV), :]
    leaves = [
        pltpu.make_async_copy(own_ref, own_hbm, sems.at[len(waits)]),
        pltpu.make_async_copy(ups_ref.at[pl.ds(HEADS_DEV, HEADS_DEV)], values_hbm, sems.at[len(waits) + 1]),
    ]
    for leave in leaves:
        leave.start()
    for wait in waits[-2:]:
        wait.wait()
    span = keys_ref.shape[2]
    lengths = lengths_ref[...]
    for seq in range(SEQS):
        blocks = []
        for keys, index in ((keys_ref, kv), (other_keys_ref, kv + 1 - 2 * core)):
            valid = index * span + iota((1, span), 1) < lengths[:, seq : seq + 1]
            scores = dot(queries[seq], keys[seq]) * SCALE + jnp.where(valid, 0.0, LOWEST)
            blocks.append((keys, valid, scores, jnp.max(scores, axis=1, keepdims=True)))
        peak = jnp.maximum(blocks[0][3], blocks[1][3])
        total, latent = 0.0, 0.0
        for keys, valid, scores, _ in blocks:
            weights = jnp.where(valid, jnp.exp(scores - peak), 0.0).astype(BF16)
            total = total + jnp.sum(weights.astype(F32), axis=1, keepdims=True)
            latent = latent + dot(weights, keys[seq, :LAT, :], NT)
        latent = latent.astype(BF16)
        stats = jnp.zeros((rows_seq, 128), F32)
        rows = slice(seq * rows_seq, (seq + 1) * rows_seq)
        for head in range(HEADS_DEV):
            place = slice(head * rows_seq, (head + 1) * rows_seq)
            value_up = ups_ref[HEADS_DEV + head].reshape(LAT, VDIM)
            out_ref[rows, head * VDIM : (head + 1) * VDIM] = dot(latent[place], value_up).astype(BF16)
            stats = with_stats(stats, head, peak[place], total[place])
        out_ref[rows, LAT:] = stats.astype(BF16)
    for leave in leaves:
        leave.wait()


def combine_kernel(parts_ref, keys_ref, own_hbm, values_hbm, out_ref, own_ref, values_ref, sems):
    fetches = [
        pltpu.make_async_copy(own_hbm, own_ref, sems.at[0]),
        pltpu.make_async_copy(values_hbm, values_ref, sems.at[1]),
    ]
    for fetch in fetches:
        fetch.start()
    kv = kv_index()
    stats = whole_stats(parts_ref[:, :, LAT:].astype(F32))
    keys = []
    for step in range(STEPS):
        block = keys_ref[step * (PAIRS // ROWS_TP) + kv // 2].astype(F32)
        keys.append(jnp.concatenate([block[:, :256], swap_halves(block[:, :256]), block[:, 256 : 256 + ROPE]], axis=1))
    keys = jnp.concatenate(keys, axis=0).astype(BF16)
    cached = []
    for head in range(HEADS_DEV):
        peak = stats[:, :, head : head + 1]
        total = stats[:, :, HEADS_DEV + head : HEADS_DEV + head + 1]
        top = jnp.max(peak, axis=0)
        keep = jnp.exp(peak - top[None])
        part = parts_ref[:, :, head * VDIM : (head + 1) * VDIM].astype(F32)
        cached.append((top, jnp.sum(part * keep, axis=0), jnp.sum(total * keep, axis=0)))
    for fetch in fetches:
        fetch.wait()
    scores = dot(own_ref[...], keys, NT) * SCALE
    row = iota(scores.shape, 0) % ROWS_KV
    key = iota(scores.shape, 1)
    causal = (row // STEPS == key % ROWS_TP) & (key // ROWS_TP <= row % STEPS)
    scores = jnp.where(causal, scores, LOWEST)
    fresh_peak = jnp.max(scores, axis=1, keepdims=True)
    weights = jnp.where(causal, jnp.exp(scores - fresh_peak), 0.0).astype(BF16)
    fresh_total = jnp.sum(weights.astype(F32), axis=1, keepdims=True)
    fresh_latent = dot(weights, keys[:, :LAT]).astype(BF16)
    for head, (peak, value, total) in enumerate(cached):
        own = slice(head * ROWS_KV, (head + 1) * ROWS_KV)
        top = jnp.maximum(peak, fresh_peak[own])
        keep, fresh_keep = jnp.exp(peak - top), jnp.exp(fresh_peak[own] - top)
        value_up = values_ref[head].reshape(LAT, VDIM)
        value = value * keep + dot(fresh_latent[own], value_up) * fresh_keep
        value = (value / (total * keep + fresh_total[own] * fresh_keep)).astype(BF16)
        for place in range(CHIPS):
            out_ref[place, :, head * VDIM : (head + 1) * VDIM] = value


def own_half(shape, dim):
    return iota(shape, dim) % ROWS_TP // (ROWS_TP // 2) == kv_index() % 2


def project_kernel(values_ref, own_ref, other_ref, out_ref):
    values = values_ref[...].reshape(CLASS, HEADS_DEV * VDIM)
    shape = (TOKROWS, CLASS)
    row, source = iota(shape, 0), iota(shape, 1)
    block, pair = row // ROWS_TP, row % (ROWS_TP // 2)
    match = source == block % CHIPS * ROWS_KV + pair * STEPS + block // CHIPS
    own = (match & own_half(shape, 0)).astype(F32).astype(BF16)
    other = (match & ~own_half(shape, 0)).astype(F32).astype(BF16)
    out = dot(dot(own, values).astype(BF16), own_ref[...], NT)
    out = out + dot(dot(other, values).astype(BF16), other_ref[...], NT)
    out_ref[...] = out.reshape(N_TP, ROWS_TP, FEAT).astype(BF16)


def route_kernel(parts_ref, mine_ref, other_ref, attended_ref, out_ref):
    attended = jnp.sum(parts_ref[...].astype(F32), axis=0).astype(BF16)
    attended_ref[...] = attended
    own = own_half((ROWS_TP, FEAT), 0)
    tokens = jnp.where(own, from_tiles(mine_ref[TOKEN_AT:, :]), swap_halves(from_tiles(other_ref[TOKEN_AT:, :])))
    gain = jnp.where(own, from_tiles(mine_ref[GAIN_AT:, :]), from_tiles(other_ref[GAIN_AT:, :]))
    mid = tokens + attended.astype(F32)
    lane = iota((ROWS_TP, 512 - FEAT), 1)
    extra = jnp.zeros(lane.shape, F32)
    for at, part in enumerate(parts_of(jnp.sum(mid * mid, axis=1, keepdims=True))):
        extra = jnp.where(lane == at, part, extra)
    row_data = jnp.concatenate([mid * gain, extra], axis=1).astype(BF16)
    for place in range(N_TP):
        out_ref[place] = row_data


def gate_kernel(
    rows_ref, other_gate_ref, other_up_ref, own_gate_hbm, own_up_hbm, out_ref, own_gate_ref, own_up_ref, sems,
):
    fetches = [
        pltpu.make_async_copy(own_gate_hbm, own_gate_ref, sems.at[0]),
        pltpu.make_async_copy(own_up_hbm, own_up_ref, sems.at[1]),
    ]
    for fetch in fetches:
        fetch.start()
    rows = rows_ref[...].astype(F32).reshape(TOKROWS, 512).astype(BF16)
    shape = (CLASS, TOKROWS)
    place, row = iota(shape, 0), iota(shape, 1)
    match = place == row // ROWS_TP * (ROWS_TP // 2) + row % (ROWS_TP // 2)
    own = dot((match & own_half(shape, 1)).astype(F32).astype(BF16), rows).astype(BF16)
    other = dot((match & ~own_half(shape, 1)).astype(F32).astype(BF16), rows).astype(BF16)
    sixteen, column = iota((16, 512), 0), iota((16, 512), 1)
    first = ((sixteen < 3) & (column == FEAT + sixteen)).astype(F32).astype(BF16)
    second = ((sixteen >= 3) & (sixteen < 6) & (column == FEAT + sixteen - 3)).astype(F32).astype(BF16)
    squares = (dot(first, own, NT) + dot(second, other, NT)).astype(BF16)
    own, other = own[:, :FEAT], other[:, :FEAT]
    gate = dot(other, other_gate_ref[0])
    up = dot(other, other_up_ref[0])
    for fetch in fetches:
        fetch.wait()
    gate = gate + dot(own, own_gate_ref[0])
    up = up + dot(own, own_up_ref[0])
    for place in range(CHIPS):
        columns = slice(place * HID_Y, (place + 1) * HID_Y)
        out_ref[place, :CLASS, :] = gate[:, columns].astype(BF16)
        out_ref[place, CLASS : 2 * CLASS, :] = up[:, columns].astype(BF16)
        out_ref[place, 2 * CLASS :, :] = squares


def hidden_kernel(parts_ref, out_ref):
    gate = jnp.sum(parts_ref[:, :CLASS, :].astype(F32), axis=0)
    up = jnp.sum(parts_ref[:, CLASS : 2 * CLASS, :].astype(F32), axis=0)
    squares = jnp.sum(parts_ref[:, 2 * CLASS :, :].astype(F32), axis=0)
    squares = jnp.sum(squares[:6], axis=0, keepdims=True)
    diagonal = iota((CLASS, CLASS), 0) == iota((CLASS, CLASS), 1)
    squares = jnp.sum(jnp.where(diagonal, squares, 0.0), axis=1, keepdims=True)
    scale = lax.rsqrt(squares / D + EPS)
    gate = gate * scale
    hidden = (gate / (1.0 + jnp.exp(-gate)) * (up * scale)).astype(BF16)
    for place in range(CHIPS):
        out_ref[place] = hidden


def down_kernel(hidden_ref, weights_ref, out_ref):
    hidden = jnp.concatenate([hidden_ref[chip] for chip in range(CHIPS)], axis=1)
    out_ref[...] = dot(hidden, weights_ref[0], NT).astype(BF16)


def join_kernel(own_ref, came_ref, out_ref):
    shape = (TOKROWS, CLASS)
    row, source = iota(shape, 0), iota(shape, 1)
    match = source == row // ROWS_TP * (ROWS_TP // 2) + row % (ROWS_TP // 2)
    own = (match & own_half(shape, 0)).astype(F32).astype(BF16)
    other = (match & ~own_half(shape, 0)).astype(F32).astype(BF16)
    out = dot(own, own_ref[...]) + dot(other, came_ref[...])
    out_ref[...] = out.reshape(N_TP, ROWS_TP, FEAT).astype(BF16)


def mix_kernel(parts_ref, mine_ref, own_ref, other_ref, ids_ref, weights_ref, attended_ref, out_ref):
    own = own_ref[...].astype(F32)
    attended = jnp.where(own_half(own.shape, 0), own, swap_halves(other_ref[...].astype(F32)))
    attended_ref[...] = attended.astype(BF16)
    total = from_tiles(mine_ref[TOKEN_AT:, :]) + attended
    ids = ids_ref[...]
    weights = weights_ref[...]
    for expert in range(EXPERTS):
        share = jnp.sum(jnp.where(ids == expert, weights, 0.0), axis=1, keepdims=True)
        both = parts_ref[2 * expert].astype(F32) + parts_ref[2 * expert + 1].astype(F32)
        total = total + share * both
    out_ref[...] = total.astype(BF16)


def run(kernel, outs, *operands, fetched=(), left=0, scratch=(), cost=None, limit=24, after=()):
    single = not isinstance(outs, list)
    outs = [outs] if single else outs
    vmem, hbm, free = (pl.BlockSpec(memory_space=space) for space in (pltpu.VMEM, pltpu.HBM, pl.ANY))
    outs = outs[: len(outs) - left] + [pltpu.HBM(out.shape, out.dtype) for out in outs[len(outs) - left :]]
    placed = [vmem] * (len(outs) - left) + [hbm] * left
    count = len(operands) + len(fetched)

    def body(*refs):
        kernel(*refs[:count], *refs[count + len(after) :])

    return pl.pallas_call(
        body,
        out_shape=outs[0] if single else tuple(outs),
        in_specs=[vmem] * len(operands) + [free] * (len(fetched) + len(after)),
        out_specs=placed[0] if single else tuple(placed),
        scratch_shapes=list(scratch),
        cost_estimate=cost,
        compiler_params=pltpu.CompilerParams(vmem_limit_bytes=limit * 2**20),
    )(*operands, *fetched, *after)


def in_hbm(array):
    return pltpu.with_memory_space_constraint(array, pltpu.HBM)


def shaped(*shape, dtype=BF16):
    return jax.ShapeDtypeStruct(shape, dtype)


def start(tokens, attn_gain, down_kv, key_up, value_up, mlp_gain):
    return run(
        start_kernel, [shaped(CHIPS, UP_ROWS + FRESH_ROWS, 128), shaped(8 * ROWS_TP, 128, dtype=F32)],
        tokens, attn_gain.reshape(1, FEAT), down_kv, jnp.swapaxes(key_up, 1, 2), value_up,
        mlp_gain.reshape(1, FEAT), limit=60,
    )


def fresh(own, other, latent_gain, lengths):
    freq = 10000.0 ** (-2.0 * jnp.arange(ROPE // 2, dtype=F32) / ROPE)
    part = pltpu.VMEM((CHIPS, FRESH_ROWS, 128), BF16)
    return run(
        fresh_kernel, shaped(N_TP, ROWS_TP, KEY_W),
        latent_gain.reshape(1, LAT), lengths.reshape(1, SEQS), freq[None], fetched=(own, other),
        left=1, scratch=[part, part, pltpu.VMEM((N_TP, ROWS_TP, KEY_W), BF16), pltpu.SemaphoreType.DMA((3,))],
    )


def attend(lengths, own, other, query_nope, query_rope, keys, other_keys):
    return run(
        attend_kernel,
        [
            shaped(CLASS, ATT_W),
            shaped(HEADS_DEV * ROWS_KV, KEY),
            shaped(HEADS_DEV, CHIPS, 2, LAT_KV, 128),
        ],
        lengths.reshape(1, SEQS),
        fetched=(in_hbm(own), in_hbm(other), in_hbm(query_nope), in_hbm(query_rope), in_hbm(keys), other_keys),
        left=2,
        scratch=[
            pltpu.VMEM((2 * HEADS_DEV, CHIPS, 2, LAT_KV, 128), BF16),
            pltpu.VMEM((HEADS_DEV * ROWS_KV, KEY), BF16),
            pltpu.VMEM((SEQS, HEADS_DEV * CLASS // SEQS, KEY), BF16),
            pltpu.VMEM(query_nope.shape, BF16),
            pltpu.VMEM(query_rope.shape, BF16),
            pltpu.VMEM(keys.shape, BF16),
            pltpu.VMEM(keys.shape, BF16),
            pltpu.SemaphoreType.DMA((6 + 4 * HEADS_DEV,)),
        ],
        cost=pl.CostEstimate(flops=2_200_000_000, bytes_accessed=4_000_000, transcendentals=800_000),
    )


def combine(parts, own, values, keys):
    return run(
        combine_kernel, shaped(CHIPS, ROWS_KV, HEADS_DEV * VDIM), parts, keys,
        fetched=(in_hbm(own), in_hbm(values)),
        scratch=[
            pltpu.VMEM(own.shape, BF16), pltpu.VMEM(values.shape, BF16), pltpu.SemaphoreType.DMA((2,)),
        ],
    )


def project(values, own, other):
    return run(project_kernel, shaped(N_TP, ROWS_TP, FEAT), values, own, other)


def route(parts, mine, other):
    return run(route_kernel, [shaped(ROWS_TP, FEAT), shaped(N_TP, ROWS_TP, 512)], parts, mine, other)


def gate(rows, own_gate, own_up, other_gate, other_up):
    weights = pltpu.VMEM(own_gate.shape, BF16)
    return run(
        gate_kernel, shaped(CHIPS, PART_ROWS, 128), rows, other_gate, other_up,
        fetched=(in_hbm(own_gate), in_hbm(own_up)), scratch=[weights, weights, pltpu.SemaphoreType.DMA((2,))],
    )


def hidden(parts):
    return run(hidden_kernel, shaped(CHIPS, CLASS, HID_Y), parts)


def down(packed, weights):
    return run(down_kernel, shaped(CLASS, FEAT), packed, weights)


def join(own, came):
    return run(join_kernel, shaped(N_TP, ROWS_TP, FEAT), own, came)


def mix(parts, mine, own, other, expert_ids, expert_weights):
    outs = [shaped(ROWS_TP, FEAT), shaped(ROWS_TP, FEAT)]
    return run(mix_kernel, outs, parts, mine, own, other, expert_ids, expert_weights)


def exchange(array, axis, groups=None):
    return lax.all_to_all(array, axis, split_axis=0, concat_axis=0, axis_index_groups=groups, tiled=True)


def along_y(array):
    return exchange(array, "kv", [[2 * chip + core for chip in range(CHIPS)] for core in range(2)])


def other_core(array):
    return lax.ppermute(array, "kv", [(index, index ^ 1) for index in range(N_KV)])


def per_device(
    tokens, attn_gain, down_kv, latent_gain, query_nope, query_rope, cache, lengths, key_up, value_up,
    out_proj, mlp_gain, expert_ids, expert_weights, gate_proj, up_proj, down_proj,
):
    ups, mine = start(tokens, attn_gain, down_kv, key_up, value_up, mlp_gain)
    own_cache, own_out, own_down = jnp.swapaxes(cache, 1, 2), out_proj.T, jnp.swapaxes(down_proj, 1, 2)
    ups, waiting, *moved = lax.optimization_barrier((ups, own_cache, gate_proj, up_proj, own_down))
    own = along_y(ups)
    other_cache = other_core(waiting)
    moved = [other_core(array) for array in moved]
    own, other_gate, other_up, other_down = lax.optimization_barrier((own, *moved))
    other = other_core(own)
    keys = fresh(own, other, latent_gain, lengths)
    keys, own, other = lax.optimization_barrier((keys, own, other))
    keys = exchange(keys, "tp")
    parts, queries, values = attend(lengths, own, other, query_nope, query_rope, own_cache, other_cache)
    parts, keys, *moved = lax.optimization_barrier((parts, keys, own_out, mine))
    other_out, other_mine = (other_core(array) for array in moved)
    parts = along_y(parts.reshape(CHIPS, ROWS_KV, ATT_W))
    values = combine(parts, queries, values, keys)
    values, other_out, other_mine = lax.optimization_barrier((values, other_out, other_mine))
    values = along_y(values)
    parts = exchange(project(values, own_out, other_out), "tp")
    attended, rows = route(parts, mine, other_mine)
    rows = exchange(rows, "tp")
    parts = along_y(gate(rows, gate_proj, up_proj, other_gate, other_up))
    packed = along_y(hidden(parts))
    came = other_core(down(packed, other_down))
    parts, leaving = lax.optimization_barrier((join(down(packed, own_down), came), attended))
    other_attended = other_core(leaving)
    parts = exchange(parts, "tp")
    return mix(parts, mine, attended, other_attended, expert_ids, expert_weights)


def solution(mesh):
    return jax.shard_map(
        per_device,
        mesh=mesh,
        in_specs=(
            P("tp", "kv"),
            P("kv"),
            P("kv", None),
            P(),
            P(None, "tp"),
            P(None, "tp"),
            P(None, "kv", None),
            P(),
            P("tp", None, "kv"),
            P("tp", "kv", None),
            P("tp", "kv"),
            P("kv"),
            P("tp", None),
            P("tp", None),
            P("tp", "kv", None),
            P("tp", "kv", None),
            P("tp", None, "kv"),
        ),
        out_specs=(P("tp", "kv"), P("tp", "kv")),
        check_vma=False,
    )
```

```python
import functools
import math

import jax
import jax.numpy as jnp
from jax import lax
from jax.experimental import pallas as pl
from jax.experimental.pallas import tpu as pltpu
from jax.sharding import PartitionSpec as P

D = 7168
NOPE = 128
ROPE = 64
LAT = 512
VDIM = 128
SEQS = 2
QROWS = 32
STEPS = 4
TOKROWS = 256
EXPERTS = 16

N_KV = 16
N_TP = 32
HEADS_DEV = 4
FEAT = D // N_KV
ROWS_TP = TOKROWS // N_TP
ROWS_KV = TOKROWS // N_KV
KEY = LAT + ROPE
PAIRS = SEQS * QROWS
STAT = 2 * HEADS_DEV
ATT_W = LAT + 128
CHIPS = N_KV // 2
LAT_KV = LAT // N_KV
UP_ROWS = 2 * HEADS_DEV * LAT_KV
FRESH_W = KEY + ROPE
FRESH_ROWS = 48
LENT_ROWS = 4 * ROWS_TP
CLASS = TOKROWS // 2
PART_ROWS = 2 * CLASS + 16
KEY_W = 384
HID = 1024
HID_Y = HID // 8

EPS = 1e-06
LOWEST = -1e30
SCALE = 1.0 / math.sqrt(NOPE + ROPE)

F32 = jnp.float32
BF16 = jnp.bfloat16
NT = (((1,), (1,)), ((), ()))
TN = (((0,), (0,)), ((), ()))


def kv_index():
    return lax.axis_index("kv")


def tp_index():
    return lax.axis_index("tp")


def iota(shape, dim):
    return lax.broadcasted_iota(jnp.int32, shape, dim)


def dot(a, b, dims=(((1,), (0,)), ((), ()))):
    return lax.dot_general(a, b, dims, preferred_element_type=F32)


def parts_of(value):
    high = value.astype(BF16).astype(F32)
    rest = value - high
    middle = rest.astype(BF16).astype(F32)
    return high, middle, rest - middle


def with_stats(stats, head, peak, total):
    lane = iota(stats.shape, 1)
    for at, part in enumerate(parts_of(peak)):
        stats = jnp.where(lane == at * STAT + head, part, stats)
    for at, part in enumerate(parts_of(total)):
        stats = jnp.where(lane == at * STAT + HEADS_DEV + head, part, stats)
    return stats


def whole_stats(tail):
    return tail[..., :STAT] + tail[..., STAT : 2 * STAT] + tail[..., 2 * STAT : 3 * STAT]


def swap_halves(rows):
    return pltpu.roll(rows, 4, 0)


def start_kernel(
    tokens_ref, gain_ref, down_ref, key_ref, value_ref, mlp_gain_ref, project_hbm, out_ref, lent_hbm, lent_ref, sems,
):
    fetch = pltpu.make_async_copy(project_hbm, lent_ref.at[pl.ds(0, FEAT), :], sems.at[0])
    fetch.start()
    wide_tokens = tokens_ref[...].astype(F32)
    mlp_gain = jnp.broadcast_to(mlp_gain_ref[...], (ROWS_TP, FEAT))
    rows = jnp.concatenate([wide_tokens, *parts_of(mlp_gain)], axis=0)
    rows = jnp.concatenate([rows, jnp.zeros((LENT_ROWS, 512 - FEAT), F32)], axis=1)
    lent_ref[FEAT:, :] = rows.astype(BF16)
    fetch.wait()
    leave = pltpu.make_async_copy(lent_ref, lent_hbm, sems.at[1])
    leave.start()
    normed = (wide_tokens * gain_ref[...]).astype(BF16)
    fresh = dot(normed, down_ref[...])
    fresh = jnp.concatenate([fresh, jnp.zeros((ROWS_TP, ROPE), F32)], axis=1)
    tiles = [fresh[:, at * 128 : (at + 1) * 128] for at in range(FRESH_W // 128)]
    tiles.append(jnp.zeros((FRESH_ROWS - ROWS_TP * len(tiles), 128), F32))
    packed = jnp.concatenate(tiles, axis=0).astype(BF16)
    for place in range(CHIPS):
        for head in range(HEADS_DEV):
            out_ref[place, head * LAT_KV : (head + 1) * LAT_KV, :] = key_ref[head]
            out_ref[place, UP_ROWS // 2 + head * LAT_KV : UP_ROWS // 2 + (head + 1) * LAT_KV, :] = value_ref[head]
        out_ref[place, UP_ROWS:, :] = packed
    leave.wait()


def fresh_kernel(gain_ref, lengths_ref, freq_ref, own_hbm, other_hbm, out_hbm, own_ref, other_ref, out_ref, sems):
    rows = pl.ds(UP_ROWS, FRESH_ROWS)
    fetches = [
        pltpu.make_async_copy(own_hbm.at[:, rows, :], own_ref, sems.at[0]),
        pltpu.make_async_copy(other_hbm.at[:, rows, :], other_ref, sems.at[1]),
    ]
    for fetch in fetches:
        fetch.start()
    for fetch in fetches:
        fetch.wait()
    packed = jnp.sum(own_ref[...].astype(F32), axis=0) + jnp.sum(other_ref[...].astype(F32), axis=0)
    tiles = [packed[at * ROWS_TP : (at + 1) * ROWS_TP] for at in range(FRESH_W // 128)]
    fresh = jnp.concatenate(tiles[:-1], axis=1)
    turn = tiles[-1][:, :ROPE]
    scaled = fresh * lax.rsqrt(jnp.mean(fresh * fresh, axis=1, keepdims=True) + EPS) * gain_ref[...]
    row = tp_index() * ROWS_TP
    lengths = lengths_ref[...]
    start = jnp.where(row // QROWS % SEQS == 0, lengths[:, 0:1], lengths[:, 1:2])
    angle = (start + row // PAIRS).astype(F32) * freq_ref[...]
    cosine, sine = jnp.cos(angle), jnp.sin(angle)
    first, second = turn[:, : ROPE // 2], turn[:, ROPE // 2 :]
    turned = [first * cosine - second * sine, second * cosine + first * sine]
    key = jnp.concatenate([scaled] + turned + [jnp.zeros((ROWS_TP, ROPE), F32)], axis=1)
    key = jnp.where(kv_index() % 2 == 0, key, swap_halves(key))
    upper = jnp.concatenate([key[:, :256], key[:, LAT:]], axis=1)
    lower = jnp.concatenate([swap_halves(key[:, 256:LAT]), jnp.zeros((ROWS_TP, KEY_W - 256), F32)], axis=1)
    key = jnp.where(iota(upper.shape, 0) < ROWS_TP // 2, upper, lower).astype(BF16)
    for place in range(N_TP):
        out_ref[place] = key
    leave = pltpu.make_async_copy(out_ref, out_hbm, sems.at[2])
    leave.start()
    leave.wait()


def attend_kernel(
    lengths_ref, own_ups_hbm, other_ups_hbm, nope_hbm, rope_hbm, keys_hbm, other_keys_hbm,
    out_ref, own_hbm, values_hbm, ups_ref, own_ref, queries, nope_ref, rope_ref, keys_ref, other_keys_ref, sems,
):
    kv = kv_index()
    core = kv % 2
    waits = []

    def fetch(source, target):
        waits.append(pltpu.make_async_copy(source, target, sems.at[len(waits)]))
        waits[-1].start()

    fetch(nope_hbm, nope_ref)
    fetch(rope_hbm, rope_ref)
    for which in range(2 * HEADS_DEV):
        rows = pl.ds(which * LAT_KV, LAT_KV)
        fetch(own_ups_hbm.at[:, rows, :], ups_ref.at[which, :, core])
        fetch(other_ups_hbm.at[:, rows, :], ups_ref.at[which, :, 1 - core])
    fetch(keys_hbm, keys_ref)
    fetch(other_keys_hbm, other_keys_ref)
    row, source = iota((CLASS, TOKROWS), 0), iota((CLASS, TOKROWS), 1)
    pair = row // ROWS_KV * ROWS_TP + core * (ROWS_TP // 2) + row % ROWS_KV // STEPS
    reorder = (source == row % STEPS * PAIRS + pair).astype(F32).astype(BF16)
    rows_seq = CLASS // SEQS
    for wait in waits[:-2]:
        wait.wait()
    nope = dot(reorder, nope_ref[...]).astype(BF16)
    rope = dot(reorder, rope_ref[...]).astype(BF16)
    for head in range(HEADS_DEV):
        key_up = ups_ref[head].reshape(LAT, NOPE)
        absorbed = dot(nope[:, head * NOPE : (head + 1) * NOPE], key_up, NT).astype(BF16)
        turned = rope[:, head * ROPE : (head + 1) * ROPE]
        for seq in range(SEQS):
            rows = slice(seq * rows_seq, (seq + 1) * rows_seq)
            place = slice(head * rows_seq, (head + 1) * rows_seq)
            queries[seq, place, :LAT] = absorbed[rows]
            queries[seq, place, LAT:] = turned[rows]
    own_seq = kv // (N_KV // SEQS)
    own_row = kv // 2 % (CHIPS // SEQS) * ROWS_KV
    for head in range(HEADS_DEV):
        begin = pl.multiple_of(head * rows_seq + own_row, ROWS_KV)
        own_ref[head * ROWS_KV : (head + 1) * ROWS_KV, :] = queries[own_seq, pl.ds(begin, ROWS_KV), :]
    leaves = [
        pltpu.make_async_copy(own_ref, own_hbm, sems.at[len(waits)]),
        pltpu.make_async_copy(ups_ref.at[pl.ds(HEADS_DEV, HEADS_DEV)], values_hbm, sems.at[len(waits) + 1]),
    ]
    for leave in leaves:
        leave.start()
    for wait in waits[-2:]:
        wait.wait()
    span = keys_ref.shape[2]
    lengths = lengths_ref[...]
    for seq in range(SEQS):
        blocks = []
        for keys, index in ((keys_ref, kv), (other_keys_ref, kv + 1 - 2 * core)):
            valid = index * span + iota((1, span), 1) < lengths[:, seq : seq + 1]
            scores = dot(queries[seq], keys[seq]) * SCALE + jnp.where(valid, 0.0, LOWEST)
            blocks.append((keys, valid, scores, jnp.max(scores, axis=1, keepdims=True)))
        peak = jnp.maximum(blocks[0][3], blocks[1][3])
        total, latent = 0.0, 0.0
        for keys, valid, scores, _ in blocks:
            weights = jnp.where(valid, jnp.exp(scores - peak), 0.0).astype(BF16)
            total = total + jnp.sum(weights.astype(F32), axis=1, keepdims=True)
            latent = latent + dot(weights, keys[seq, :LAT, :], NT)
        latent = latent.astype(BF16)
        stats = jnp.zeros((rows_seq, 128), F32)
        rows = slice(seq * rows_seq, (seq + 1) * rows_seq)
        for head in range(HEADS_DEV):
            place = slice(head * rows_seq, (head + 1) * rows_seq)
            value_up = ups_ref[HEADS_DEV + head].reshape(LAT, VDIM)
            out_ref[rows, head * VDIM : (head + 1) * VDIM] = dot(latent[place], value_up).astype(BF16)
            stats = with_stats(stats, head, peak[place], total[place])
        out_ref[rows, LAT:] = stats.astype(BF16)
    for leave in leaves:
        leave.wait()


def combine_kernel(parts_ref, keys_ref, own_hbm, values_hbm, out_ref, own_ref, values_ref, sems):
    fetches = [
        pltpu.make_async_copy(own_hbm, own_ref, sems.at[0]),
        pltpu.make_async_copy(values_hbm, values_ref, sems.at[1]),
    ]
    for fetch in fetches:
        fetch.start()
    kv = kv_index()
    stats = whole_stats(parts_ref[:, :, LAT:].astype(F32))
    keys = []
    for step in range(STEPS):
        block = keys_ref[step * (PAIRS // ROWS_TP) + kv // 2].astype(F32)
        keys.append(jnp.concatenate([block[:, :256], swap_halves(block[:, :256]), block[:, 256 : 256 + ROPE]], axis=1))
    keys = jnp.concatenate(keys, axis=0).astype(BF16)
    cached = []
    for head in range(HEADS_DEV):
        peak = stats[:, :, head : head + 1]
        total = stats[:, :, HEADS_DEV + head : HEADS_DEV + head + 1]
        top = jnp.max(peak, axis=0)
        keep = jnp.exp(peak - top[None])
        part = parts_ref[:, :, head * VDIM : (head + 1) * VDIM].astype(F32)
        cached.append((top, jnp.sum(part * keep, axis=0), jnp.sum(total * keep, axis=0)))
    for fetch in fetches:
        fetch.wait()
    scores = dot(own_ref[...], keys, NT) * SCALE
    row = iota(scores.shape, 0) % ROWS_KV
    key = iota(scores.shape, 1)
    causal = (row // STEPS == key % ROWS_TP) & (key // ROWS_TP <= row % STEPS)
    scores = jnp.where(causal, scores, LOWEST)
    fresh_peak = jnp.max(scores, axis=1, keepdims=True)
    weights = jnp.where(causal, jnp.exp(scores - fresh_peak), 0.0).astype(BF16)
    fresh_total = jnp.sum(weights.astype(F32), axis=1, keepdims=True)
    fresh_latent = dot(weights, keys[:, :LAT]).astype(BF16)
    for head, (peak, value, total) in enumerate(cached):
        own = slice(head * ROWS_KV, (head + 1) * ROWS_KV)
        top = jnp.maximum(peak, fresh_peak[own])
        keep, fresh_keep = jnp.exp(peak - top), jnp.exp(fresh_peak[own] - top)
        value_up = values_ref[head].reshape(LAT, VDIM)
        value = value * keep + dot(fresh_latent[own], value_up) * fresh_keep
        value = (value / (total * keep + fresh_total[own] * fresh_keep)).astype(BF16)
        for place in range(CHIPS):
            out_ref[place, :, head * VDIM : (head + 1) * VDIM] = value


def own_half(shape, dim):
    return iota(shape, dim) % ROWS_TP // (ROWS_TP // 2) == kv_index() % 2


def project_kernel(values_ref, own_ref, other_ref, out_ref):
    values = values_ref[...].reshape(CLASS, HEADS_DEV * VDIM)
    shape = (TOKROWS, CLASS)
    row, source = iota(shape, 0), iota(shape, 1)
    block, pair = row // ROWS_TP, row % (ROWS_TP // 2)
    match = source == block % CHIPS * ROWS_KV + pair * STEPS + block // CHIPS
    own = (match & own_half(shape, 0)).astype(F32).astype(BF16)
    other = (match & ~own_half(shape, 0)).astype(F32).astype(BF16)
    out = dot(dot(own, values).astype(BF16), own_ref[...], NT)
    out = out + dot(dot(other, values).astype(BF16), other_ref[:FEAT, :], NT)
    out_ref[...] = out.reshape(N_TP, ROWS_TP, FEAT).astype(BF16)


def route_kernel(parts_ref, tokens_ref, gain_ref, lent_ref, attended_ref, out_ref):
    attended = jnp.sum(parts_ref[...].astype(F32), axis=0).astype(BF16)
    attended_ref[...] = attended
    own = own_half((ROWS_TP, FEAT), 0)
    lent = lent_ref[FEAT:, :].astype(F32)[:, :FEAT]
    tokens = jnp.where(own, tokens_ref[...].astype(F32), swap_halves(lent[:ROWS_TP]))
    gain = lent[ROWS_TP : 2 * ROWS_TP] + lent[2 * ROWS_TP : 3 * ROWS_TP] + lent[3 * ROWS_TP :]
    gain = jnp.where(own, gain_ref[...], gain)
    mid = tokens + attended.astype(F32)
    lane = iota((ROWS_TP, 512 - FEAT), 1)
    extra = jnp.zeros(lane.shape, F32)
    for at, part in enumerate(parts_of(jnp.sum(mid * mid, axis=1, keepdims=True))):
        extra = jnp.where(lane == at, part, extra)
    row_data = jnp.concatenate([mid * gain, extra], axis=1).astype(BF16)
    for place in range(N_TP):
        out_ref[place] = row_data


def gate_kernel(
    rows_ref, other_gate_ref, other_up_ref, own_gate_hbm, own_up_hbm, out_ref, own_gate_ref, own_up_ref, sems,
):
    fetches = [
        pltpu.make_async_copy(own_gate_hbm, own_gate_ref, sems.at[0]),
        pltpu.make_async_copy(own_up_hbm, own_up_ref, sems.at[1]),
    ]
    for fetch in fetches:
        fetch.start()
    rows = rows_ref[...].astype(F32).reshape(TOKROWS, 512).astype(BF16)
    shape = (CLASS, TOKROWS)
    place, row = iota(shape, 0), iota(shape, 1)
    match = place == row // ROWS_TP * (ROWS_TP // 2) + row % (ROWS_TP // 2)
    own = dot((match & own_half(shape, 1)).astype(F32).astype(BF16), rows).astype(BF16)
    other = dot((match & ~own_half(shape, 1)).astype(F32).astype(BF16), rows).astype(BF16)
    sixteen, column = iota((16, 512), 0), iota((16, 512), 1)
    first = ((sixteen < 3) & (column == FEAT + sixteen)).astype(F32).astype(BF16)
    second = ((sixteen >= 3) & (sixteen < 6) & (column == FEAT + sixteen - 3)).astype(F32).astype(BF16)
    squares = (dot(first, own, NT) + dot(second, other, NT)).astype(BF16)
    own, other = own[:, :FEAT], other[:, :FEAT]
    gate = dot(other, other_gate_ref[0])
    up = dot(other, other_up_ref[0])
    for fetch in fetches:
        fetch.wait()
    gate = gate + dot(own, own_gate_ref[0])
    up = up + dot(own, own_up_ref[0])
    for place in range(CHIPS):
        columns = slice(place * HID_Y, (place + 1) * HID_Y)
        out_ref[place, :CLASS, :] = gate[:, columns].astype(BF16)
        out_ref[place, CLASS : 2 * CLASS, :] = up[:, columns].astype(BF16)
        out_ref[place, 2 * CLASS :, :] = squares


def hidden_kernel(parts_ref, out_ref):
    gate = jnp.sum(parts_ref[:, :CLASS, :].astype(F32), axis=0)
    up = jnp.sum(parts_ref[:, CLASS : 2 * CLASS, :].astype(F32), axis=0)
    squares = jnp.sum(parts_ref[:, 2 * CLASS :, :].astype(F32), axis=0)
    squares = jnp.sum(squares[:6], axis=0, keepdims=True)
    diagonal = iota((CLASS, CLASS), 0) == iota((CLASS, CLASS), 1)
    squares = jnp.sum(jnp.where(diagonal, squares, 0.0), axis=1, keepdims=True)
    scale = lax.rsqrt(squares / D + EPS)
    gate = gate * scale
    hidden = (gate / (1.0 + jnp.exp(-gate)) * (up * scale)).astype(BF16)
    for place in range(CHIPS):
        out_ref[place] = hidden


def down_kernel(hidden_ref, weights_ref, out_ref):
    hidden = jnp.concatenate([hidden_ref[chip] for chip in range(CHIPS)], axis=1)
    out_ref[...] = dot(hidden, weights_ref[0], NT).astype(BF16)


def join_kernel(own_ref, came_ref, out_ref):
    shape = (TOKROWS, CLASS)
    row, source = iota(shape, 0), iota(shape, 1)
    match = source == row // ROWS_TP * (ROWS_TP // 2) + row % (ROWS_TP // 2)
    own = (match & own_half(shape, 0)).astype(F32).astype(BF16)
    other = (match & ~own_half(shape, 0)).astype(F32).astype(BF16)
    out = dot(own, own_ref[...]) + dot(other, came_ref[...])
    out_ref[...] = out.reshape(N_TP, ROWS_TP, FEAT).astype(BF16)


def mix_kernel(parts_ref, tokens_ref, own_ref, other_ref, ids_ref, weights_ref, attended_ref, out_ref):
    own = own_ref[...].astype(F32)
    attended = jnp.where(own_half(own.shape, 0), own, swap_halves(other_ref[...].astype(F32)))
    attended_ref[...] = attended.astype(BF16)
    total = tokens_ref[...].astype(F32) + attended
    ids = ids_ref[...]
    weights = weights_ref[...]
    for expert in range(EXPERTS):
        share = jnp.sum(jnp.where(ids == expert, weights, 0.0), axis=1, keepdims=True)
        both = parts_ref[2 * expert].astype(F32) + parts_ref[2 * expert + 1].astype(F32)
        total = total + share * both
    out_ref[...] = total.astype(BF16)


def run(kernel, outs, *operands, fetched=(), left=0, scratch=(), cost=None, limit=24, after=()):
    single = not isinstance(outs, list)
    outs = [outs] if single else outs
    vmem, hbm, free = (pl.BlockSpec(memory_space=space) for space in (pltpu.VMEM, pltpu.HBM, pl.ANY))
    outs = outs[: len(outs) - left] + [pltpu.HBM(out.shape, out.dtype) for out in outs[len(outs) - left :]]
    placed = [vmem] * (len(outs) - left) + [hbm] * left
    count = len(operands) + len(fetched)

    def body(*refs):
        kernel(*refs[:count], *refs[count + len(after) :])

    return pl.pallas_call(
        body,
        out_shape=outs[0] if single else tuple(outs),
        in_specs=[vmem] * len(operands) + [free] * (len(fetched) + len(after)),
        out_specs=placed[0] if single else tuple(placed),
        scratch_shapes=list(scratch),
        cost_estimate=cost,
        compiler_params=pltpu.CompilerParams(vmem_limit_bytes=limit * 2**20),
    )(*operands, *fetched, *after)


def in_hbm(array):
    return pltpu.with_memory_space_constraint(array, pltpu.HBM)


def shaped(*shape, dtype=BF16):
    return jax.ShapeDtypeStruct(shape, dtype)


def start(tokens, attn_gain, down_kv, key_up, value_up, mlp_gain, project_weights):
    return run(
        start_kernel, [shaped(CHIPS, UP_ROWS + FRESH_ROWS, 128), shaped(FEAT + LENT_ROWS, 512)],
        tokens, attn_gain.reshape(1, FEAT), down_kv, jnp.swapaxes(key_up, 1, 2), value_up, mlp_gain.reshape(1, FEAT),
        fetched=(in_hbm(project_weights),), left=1, limit=60,
        scratch=[pltpu.VMEM((FEAT + LENT_ROWS, 512), BF16), pltpu.SemaphoreType.DMA((2,))],
    )


def fresh(own, other, latent_gain, lengths):
    freq = 10000.0 ** (-2.0 * jnp.arange(ROPE // 2, dtype=F32) / ROPE)
    part = pltpu.VMEM((CHIPS, FRESH_ROWS, 128), BF16)
    return run(
        fresh_kernel, shaped(N_TP, ROWS_TP, KEY_W),
        latent_gain.reshape(1, LAT), lengths.reshape(1, SEQS), freq[None], fetched=(own, other),
        left=1, scratch=[part, part, pltpu.VMEM((N_TP, ROWS_TP, KEY_W), BF16), pltpu.SemaphoreType.DMA((3,))],
    )


def attend(lengths, own, other, query_nope, query_rope, keys, other_keys):
    return run(
        attend_kernel,
        [
            shaped(CLASS, ATT_W),
            shaped(HEADS_DEV * ROWS_KV, KEY),
            shaped(HEADS_DEV, CHIPS, 2, LAT_KV, 128),
        ],
        lengths.reshape(1, SEQS),
        fetched=(in_hbm(own), in_hbm(other), in_hbm(query_nope), in_hbm(query_rope), in_hbm(keys), other_keys),
        left=2,
        scratch=[
            pltpu.VMEM((2 * HEADS_DEV, CHIPS, 2, LAT_KV, 128), BF16),
            pltpu.VMEM((HEADS_DEV * ROWS_KV, KEY), BF16),
            pltpu.VMEM((SEQS, HEADS_DEV * CLASS // SEQS, KEY), BF16),
            pltpu.VMEM(query_nope.shape, BF16),
            pltpu.VMEM(query_rope.shape, BF16),
            pltpu.VMEM(keys.shape, BF16),
            pltpu.VMEM(keys.shape, BF16),
            pltpu.SemaphoreType.DMA((6 + 4 * HEADS_DEV,)),
        ],
        cost=pl.CostEstimate(flops=2_200_000_000, bytes_accessed=4_000_000, transcendentals=800_000),
    )


def combine(parts, own, values, keys):
    return run(
        combine_kernel, shaped(CHIPS, ROWS_KV, HEADS_DEV * VDIM), parts, keys,
        fetched=(in_hbm(own), in_hbm(values)),
        scratch=[
            pltpu.VMEM(own.shape, BF16), pltpu.VMEM(values.shape, BF16), pltpu.SemaphoreType.DMA((2,)),
        ],
    )


def project(values, own, other):
    return run(project_kernel, shaped(N_TP, ROWS_TP, FEAT), values, own, other)


def route(parts, tokens, mlp_gain, lent):
    outs = [shaped(ROWS_TP, FEAT), shaped(N_TP, ROWS_TP, 512)]
    return run(route_kernel, outs, parts, tokens, mlp_gain.reshape(1, FEAT), lent)


def gate(rows, own_gate, own_up, other_gate, other_up):
    weights = pltpu.VMEM(own_gate.shape, BF16)
    return run(
        gate_kernel, shaped(CHIPS, PART_ROWS, 128), rows, other_gate, other_up,
        fetched=(in_hbm(own_gate), in_hbm(own_up)), scratch=[weights, weights, pltpu.SemaphoreType.DMA((2,))],
    )


def hidden(parts):
    return run(hidden_kernel, shaped(CHIPS, CLASS, HID_Y), parts)


def down(packed, weights):
    return run(down_kernel, shaped(CLASS, FEAT), packed, weights)


def join(own, came):
    return run(join_kernel, shaped(N_TP, ROWS_TP, FEAT), own, came)


def mix(parts, tokens, own, other, expert_ids, expert_weights):
    outs = [shaped(ROWS_TP, FEAT), shaped(ROWS_TP, FEAT)]
    return run(mix_kernel, outs, parts, tokens, own, other, expert_ids, expert_weights)


def exchange(array, axis, groups=None):
    return lax.all_to_all(array, axis, split_axis=0, concat_axis=0, axis_index_groups=groups, tiled=True)


def along_y(array):
    return exchange(array, "kv", [[2 * chip + core for chip in range(CHIPS)] for core in range(2)])


def other_core(array):
    return lax.ppermute(array, "kv", [(index, index ^ 1) for index in range(N_KV)])


def per_device(
    tokens, attn_gain, down_kv, latent_gain, query_nope, query_rope, cache, lengths, key_up, value_up,
    out_proj, mlp_gain, expert_ids, expert_weights, gate_proj, up_proj, down_proj,
):
    own_cache, own_out, own_down = jnp.swapaxes(cache, 1, 2), out_proj.T, jnp.swapaxes(down_proj, 1, 2)
    ups, lent = start(tokens, attn_gain, down_kv, key_up, value_up, mlp_gain, own_out)
    ups, waiting, *moved = lax.optimization_barrier((ups, own_cache, lent, gate_proj, up_proj, own_down))
    own = along_y(ups)
    other_cache = other_core(waiting)
    moved = [other_core(array) for array in moved]
    own, lent, other_gate, other_up, other_down = lax.optimization_barrier((own, *moved))
    other = other_core(own)
    keys = fresh(own, other, latent_gain, lengths)
    keys, own, other = lax.optimization_barrier((keys, own, other))
    keys = exchange(keys, "tp")
    parts, queries, values = attend(lengths, own, other, query_nope, query_rope, own_cache, other_cache)
    parts, keys = lax.optimization_barrier((parts, keys))
    parts = along_y(parts.reshape(CHIPS, ROWS_KV, ATT_W))
    values = along_y(combine(parts, queries, values, keys))
    parts = exchange(project(values, own_out, lent), "tp")
    attended, rows = route(parts, tokens, mlp_gain, lent)
    rows = exchange(rows, "tp")
    parts = along_y(gate(rows, gate_proj, up_proj, other_gate, other_up))
    packed = along_y(hidden(parts))
    came = other_core(down(packed, other_down))
    parts, leaving = lax.optimization_barrier((join(down(packed, own_down), came), attended))
    other_attended = other_core(leaving)
    parts = exchange(parts, "tp")
    return mix(parts, tokens, attended, other_attended, expert_ids, expert_weights)


def solution(mesh):
    return jax.shard_map(
        per_device,
        mesh=mesh,
        in_specs=(
            P("tp", "kv"),
            P("kv"),
            P("kv", None),
            P(),
            P(None, "tp"),
            P(None, "tp"),
            P(None, "kv", None),
            P(),
            P("tp", None, "kv"),
            P("tp", "kv", None),
            P("tp", "kv"),
            P("kv"),
            P("tp", None),
            P("tp", None),
            P("tp", "kv", None),
            P("tp", "kv", None),
            P("tp", None, "kv"),
        ),
        out_specs=(P("tp", "kv"), P("tp", "kv")),
        check_vma=False,
    )
```
